256 devices in a mesh: atoms: 128 (over z, y, x), chan: 2 (over core).
Axes of the slice: x: 4, y: 4, z: 8, core: 2. Of those that a mesh axis runs over, the one named last changes fastest.
Arguments:
- features: bfloat16 [4096, 6400], P('atoms', 'chan'), may hold values from -6 to 6
- send_rows: int32 [512, 32], P('atoms'), may hold values from 0 to 31
- edge_source: int32 [65536], P(('atoms', 'chan')), may hold values from 0 to 159
- edge_dest: int32 [65536], P(('atoms', 'chan')), may hold values from 0 to 32, as said below
- edge_rot: int32 [65536], P(('atoms', 'chan')), may hold values from 0 to 511
- edge_weight: float32 [65536], P(('atoms', 'chan')), may hold values from 0.25 to 1
- rot_table: float32 [512, 165], replicated, may hold values from -2.5 to 2.5
- mix_zero: bfloat16 [640, 640], replicated, may hold values from -0.25 to 0.25
- mix_one: bfloat16 [2, 512, 512], replicated, may hold values from -0.1875 to 0.1875
- mix_two: bfloat16 [2, 384, 384], replicated, may hold values from -0.21875 to 0.21875
- atom_species: int32 [4096], P('atoms'), may hold values from 0 to 3
- species_orbitals: int32 [4], replicated, may hold values from 2 to 16, as said below
- head_weight: bfloat16 [6400, 512], P(None, 'chan'), may hold values from -0.078125 to 0.078125
- target_blocks: float32 [4096, 512], P('atoms', 'chan'), may hold values from -6 to 6
Outputs:
- atom_loss: float32 [4096], P('atoms')
- grad_head: bfloat16 [6400, 512], P(None, 'chan')
- grad_features: float32 [4096, 6400], P('atoms', 'chan')
The draws below stay inside these ranges and needn't reach their ends.
Inputs may be any that keep to these rules, and one draw needn't show every extreme that they name: edge_dest == 32 marks an empty edge slot; live slots come first on each device, and some device has all 256 slots live. `species_orbitals`: each value is even; some species has 16, another 16 - 2.
All inputs are finite; a program needn't handle non-finite values.
Results may differ from the reference program's by a relative error of at most 0.0057.
Values may be sent and summed in bfloat16 or wider, within the bound.
No kernel may reach another device: no remote copies, remote signals or barrier semaphores. Data moves between devices by JAX's collectives and lax.ppermute only.
A program may use at most 128 MiB of HBM per device.

```python
import math
import jax
import jax.numpy as jnp
import numpy as np
from jax import lax

C = 128
ORB = 16
SPECIES = 4
A_DEV = 32
EDGES_DEV = 256
SLOTS = 32
ROTS = 512
HB = 512
ATOMS = 4096
EDGES = 65536
ROWS = 160
N_ATOMS = 128
N_CHAN = 2


lmax_value = 4


def packed_pattern():
    diag_flags = []
    block_widths = []
    for degree in range(lmax_value + 1):
        size_l = 2 * degree + 1
        for row_pos in range(size_l):
            for column in range(size_l):
                diag_flags.append(1.0 if row_pos == column else 0.0)
                block_widths.append(float(size_l))
    return (np.array(diag_flags, np.float32), np.array(block_widths, np.float32))


def draw_rot_table(key, part):
    key = jax.random.fold_in(key, 11)
    diag_flags, block_widths = packed_pattern()
    noise_key, scale_key = jax.random.split(key)
    noise_draw = jnp.clip(jax.random.normal(noise_key, (ROTS, diag_flags.shape[0]), jnp.float32), -3.0, 3.0) * 0.7
    factor = jnp.ones((ROTS, 1), jnp.float32)
    return jnp.asarray(diag_flags) + factor * 0.6 * noise_draw / jnp.sqrt(jnp.asarray(block_widths))


def draw_edge_dest(key, part):
    key = jax.random.fold_in(key, 23)
    count_key, dest_key, full_key = jax.random.split(key, 3)
    device_blocks = EDGES // EDGES_DEV
    counts = jax.random.randint(count_key, (device_blocks,), EDGES_DEV // 5, EDGES_DEV + 1)
    full_block = jax.random.randint(full_key, (), 0, device_blocks)
    counts = jnp.where(jnp.arange(device_blocks) == full_block, EDGES_DEV, counts)
    places = jnp.arange(EDGES_DEV)
    live_slot = places[None, :] < counts[:, None]
    dest_draw = jax.random.randint(dest_key, (device_blocks, EDGES_DEV), 0, A_DEV)
    return jnp.where(live_slot, dest_draw, A_DEV).reshape(EDGES).astype(jnp.int32)


def draw_species_orbitals(key, part):
    key = jax.random.fold_in(key, 37)
    pick_key, order_key = jax.random.split(key)
    counts = 2 * jax.random.randint(pick_key, (SPECIES,), 1, ORB // 2 + 1)
    order = jax.random.permutation(order_key, SPECIES)
    places = jnp.arange(SPECIES)
    counts = jnp.where(places == order[0], ORB, counts)
    counts = jnp.where(places == order[1], ORB - 2, counts)
    return counts.astype(jnp.int32)


def touch_ends(values, key, low, largest):
    spot = [jax.random.randint(jax.random.fold_in(key, axis), (), 0, length) for axis, length in enumerate(values.shape)]
    longest = values.shape.index(max(values.shape))
    beside = spot[:longest] + [(spot[longest] + 1) % values.shape[longest]] + spot[longest + 1:]
    return values.at[tuple(spot)].set(low).at[tuple(beside)].set(largest)


def steps_of(key, extent, cuts, least, high):
    gain, own = 1.0, jax.random.fold_in(key, 6)
    for axis_at, shards_of in cuts:
        steps = jnp.exp(jax.random.uniform(jax.random.fold_in(own, axis_at), (shards_of,), jnp.float32, least / len(cuts), high / len(cuts)))
        gain = gain * jnp.repeat(steps, extent[axis_at] // shards_of).reshape([-1 if axis == axis_at else 1 for axis in range(len(extent))])
    return gain


def bell_draw(own_key, dims, scale, bound, cuts=(), kind=jnp.bfloat16):
    drawn = jax.random.normal(own_key, dims, jnp.float32) * scale
    if len(cuts) > 0:
        drawn = steps_of(own_key, dims, cuts, -0.22, 0.18) * drawn
    return jnp.clip(drawn, min=-bound, max=bound).astype(kind)


def setup_inputs(seed: int = 0) -> dict:
    arg_keys = jax.random.split(jax.random.key(seed), 15)
    features = bell_draw(arg_keys[0], (ATOMS, C * 50), 1.0, 6.0, ((0, 128), (1, 2)))
    send_rows = touch_ends(jax.random.randint(arg_keys[1], (4 * N_ATOMS, SLOTS), 0, A_DEV), jax.random.fold_in(arg_keys[1], 1), 0, A_DEV - 1).astype(jnp.int32)
    edge_source = touch_ends(jax.random.randint(arg_keys[2], (EDGES,), 0, ROWS), jax.random.fold_in(arg_keys[2], 1), 0, ROWS - 1).astype(jnp.int32)
    edge_dest = draw_edge_dest(jax.random.fold_in(arg_keys[14], 71), 0)
    edge_rot = touch_ends(jax.random.randint(arg_keys[4], (EDGES,), 0, ROTS), jax.random.fold_in(arg_keys[4], 1), 0, ROTS - 1).astype(jnp.int32)
    edge_weight = jnp.clip(jnp.exp(math.log(1.0) - 1.3862944 * jax.random.uniform(arg_keys[5], (EDGES,), jnp.float32) ** steps_of(arg_keys[5], (EDGES,), ((0, 256),), -0.2, 0.2)), 0.25, 1.0)
    rot_table = draw_rot_table(jax.random.fold_in(arg_keys[14], 71), 0)
    mix_zero = bell_draw(arg_keys[7], (5 * C, 5 * C), (5 * C) ** -0.5, 0.25)
    mix_one = bell_draw(arg_keys[8], (2, 4 * C, 4 * C), (8 * C) ** -0.5, 0.1875)
    mix_two = bell_draw(arg_keys[9], (2, 3 * C, 3 * C), (6 * C) ** -0.5, 0.21875)
    atom_species = touch_ends(jax.random.randint(arg_keys[10], (ATOMS,), 0, SPECIES), jax.random.fold_in(arg_keys[10], 1), 0, SPECIES - 1).astype(jnp.int32)
    species_orbitals = draw_species_orbitals(jax.random.fold_in(arg_keys[14], 71), 0)
    head_weight = bell_draw(arg_keys[12], (C * 50, HB), (50 * C) ** -0.5, 0.078125, ((1, 2),))
    target_blocks = bell_draw(arg_keys[13], (ATOMS, HB), 1.0, 6.0, ((0, 128), (1, 2)), jnp.float32)
    return {"features": features, "send_rows": send_rows, "edge_source": edge_source, "edge_dest": edge_dest, "edge_rot": edge_rot, "edge_weight": edge_weight, "rot_table": rot_table, "mix_zero": mix_zero, "mix_one": mix_one, "mix_two": mix_two, "atom_species": atom_species, "species_orbitals": species_orbitals, "head_weight": head_weight, "target_blocks": target_blocks}


lmax_value = 4
mmax_value = 2
branch_scale = 0.125
shift_offsets = (1, -1, 2, -2)
highest = lax.Precision.HIGHEST


def coefficient_tables():
    retained = []
    for degree in range(lmax_value + 1):
        m_top = min(degree, mmax_value)
        for m_order in range(-m_top, m_top + 1):
            retained.append((degree, m_order))
    starts = [0]
    for degree in range(lmax_value + 1):
        starts.append(starts[-1] + (2 * degree + 1) ** 2)
    lookup = np.full((len(retained), (lmax_value + 1) ** 2), starts[-1], dtype=np.int32)
    for row_pos, pair in enumerate(retained):
        degree, m_order = pair
        size_l = 2 * degree + 1
        for column in range(size_l):
            lookup[row_pos, degree * degree + column] = starts[degree] + (degree + m_order) * size_l + column
    groups = []
    for m_order in range(mmax_value + 1):
        plus_side = [row_pos for row_pos, pair in enumerate(retained) if pair[1] == m_order]
        minus_side = [row_pos for row_pos, pair in enumerate(retained) if pair[1] == -m_order]
        groups.append((plus_side, minus_side))
    return lookup, groups


def edge_frames(rot_table, rot_ids):
    lookup = coefficient_tables()[0]
    packed = jnp.take(rot_table, rot_ids, axis=0)
    padded = jnp.concatenate([packed, jnp.zeros((packed.shape[0], 1), jnp.float32)], axis=1)
    return jnp.take(padded, jnp.asarray(lookup), axis=1)


def rotate_in(source, frames):
    return jnp.einsum("eik,ecpk->ecpi", frames, source.astype(jnp.float32), precision=highest).astype(jnp.bfloat16)


def mixing_step(rotated, mix_zero, mix_one, mix_two):
    edge_count = rotated.shape[0]
    channels = rotated.shape[1]
    groups = coefficient_tables()[1]

    def flatten(positions):
        selected = rotated[:, :, :, np.array(positions)]
        return jnp.transpose(selected, (0, 2, 1, 3)).reshape(edge_count * 2, channels * len(positions))

    def unflatten(values, width_count):
        return values.reshape(edge_count, 2, channels, width_count)

    zero_side = groups[0][0]
    pieces = [unflatten(jnp.dot(flatten(zero_side), mix_zero, preferred_element_type=jnp.float32), len(zero_side))]
    placed = list(zero_side)
    for m_order, mix_pair in ((1, mix_one), (2, mix_two)):
        plus_side, minus_side = groups[m_order]
        plus_in = flatten(plus_side)
        minus_in = flatten(minus_side)
        plus_out = jnp.dot(plus_in, mix_pair[0], preferred_element_type=jnp.float32) - jnp.dot(minus_in, mix_pair[1], preferred_element_type=jnp.float32)
        minus_out = jnp.dot(minus_in, mix_pair[0], preferred_element_type=jnp.float32) + jnp.dot(plus_in, mix_pair[1], preferred_element_type=jnp.float32)
        pieces.append(unflatten(plus_out, len(plus_side)))
        pieces.append(unflatten(minus_out, len(minus_side)))
        placed = placed + list(plus_side) + list(minus_side)
    joined = jnp.concatenate(pieces, axis=3)
    inverse = np.argsort(np.array(placed))
    return jnp.transpose(joined[:, :, :, inverse], (0, 2, 1, 3))


def rotate_out(mixture, frames, weights):
    scaled = mixture * weights[:, None, None, None]
    back = jnp.einsum("eik,ecpi->ecpk", frames, scaled, precision=highest)
    return back.reshape(back.shape[0], -1)


def reference(features, send_rows, edge_source, edge_dest, edge_rot, edge_weight, rot_table, mix_zero, mix_one, mix_two, atom_species, species_orbitals, head_weight, target_blocks):
    shards = N_ATOMS
    full_width = features.shape[1]
    channels = full_width // 50
    shard_edges = EDGES_DEV * N_CHAN
    per_shard = features.reshape(shards, A_DEV, full_width)
    send_tables = send_rows.reshape(shards, 4, SLOTS)
    sources = edge_source.reshape(shards, shard_edges)
    destinations = edge_dest.reshape(shards, shard_edges)
    rotations = edge_rot.reshape(shards, shard_edges)
    envelopes = edge_weight.reshape(shards, shard_edges)
    species = atom_species.reshape(shards, A_DEV)
    targets = target_blocks.reshape(shards, A_DEV, HB)
    columns = jnp.arange(HB, dtype=jnp.int32)
    atom_ids = jnp.arange(A_DEV, dtype=jnp.int32)
    species_ids = jnp.arange(SPECIES, dtype=jnp.int32)

    def one_shard(running, shard_pos):
        arrivals = [per_shard[shard_pos]]
        for position, offset in enumerate(shift_offsets):
            sender = (shard_pos - offset) % shards
            arrivals.append(jnp.take(per_shard[sender], send_tables[sender, position], axis=0))
        buffer_rows = jnp.concatenate(arrivals, axis=0)
        frames = edge_frames(rot_table, rotations[shard_pos])
        picked = jnp.take(buffer_rows, sources[shard_pos], axis=0).reshape(shard_edges, channels, 2, 25)
        rotated = rotate_in(picked, frames)
        mixture = mixing_step(rotated, mix_zero, mix_one, mix_two)
        messages = rotate_out(mixture, frames, envelopes[shard_pos])
        onehot = (destinations[shard_pos][None, :] == atom_ids[:, None]).astype(jnp.float32)
        aggregate = jnp.dot(onehot, messages, precision=highest, preferred_element_type=jnp.float32)
        updated = (per_shard[shard_pos].astype(jnp.float32) + branch_scale * aggregate).astype(jnp.bfloat16)
        blocks = jnp.dot(updated, head_weight, preferred_element_type=jnp.float32)
        norbitals = jnp.sum(jnp.where(species[shard_pos][:, None] == species_ids[None, :], species_orbitals[None, :], 0), axis=1)
        valid_entry = ((columns // (2 * ORB))[None, :] < norbitals[:, None]) & (((columns // 2) % ORB)[None, :] < norbitals[:, None])
        block_error = jnp.where(valid_entry, blocks - targets[shard_pos], 0.0)
        divisor = norbitals.astype(jnp.float32)
        losses = jnp.sum(block_error * block_error, axis=1) / divisor
        dblocks = (2.0 * block_error / divisor[:, None]).astype(jnp.bfloat16)
        grad_part = lax.dot_general(updated, dblocks, (((0,), (0,)), ((), ())), preferred_element_type=jnp.float32)
        feature_part = lax.dot_general(dblocks, head_weight, (((1,), (1,)), ((), ())), preferred_element_type=jnp.float32)
        return running + grad_part, (losses, feature_part)

    head_total, outputs = lax.scan(one_shard, jnp.zeros((full_width, HB), jnp.float32), jnp.arange(shards, dtype=jnp.int32))
    losses_all, feature_all = outputs
    return losses_all.reshape(ATOMS), head_total.astype(jnp.bfloat16), feature_all.reshape(ATOMS, full_width)
```

```python
import functools
import jax
import jax.numpy as jnp
import numpy as np
from jax import lax
from jax.experimental import pallas as pl
from jax.experimental.pallas import tpu as pltpu
from jax.sharding import Mesh, PartitionSpec as P

ORB = 16
LMAX = 4
MMAX = 2
OFFSETS = (1, -1, 2, -2)
BRANCH = 0.125
GROUP = ("zl", "y", "x")
ATOMS = ("zh", "zl", "y", "x")
F32 = jnp.float32
BF16 = jnp.bfloat16


def frame_entries():
    slots = {}
    start = 0
    for l in range(LMAX + 1):
        width = 2 * l + 1
        for m in range(-min(l, MMAX), min(l, MMAX) + 1):
            for n in range(width):
                slots[(l, m, n)] = (len(slots), start + (l + m) * width + n)
        start += width * width
    return slots


SLOTS = frame_entries()


def dot(a, b, ca, cb):
    return lax.dot_general(a, b, (((ca,), (cb,)), ((), ())), preferred_element_type=F32)


def message_kernel(
    core_ref, esrc_ref, edst_ref, erot_ref, ew_ref, rot_ref,
    mix0_ref, mix1_ref, mix2_ref,
    fo_ref, ho0_ref, ho1_ref, ho2_ref, ho3_ref,
    fx_ref, hx0_ref, hx1_ref, hx2_ref, hx3_ref,
    out_ref,
    rows, nat, frames, wframes, packed, z0, z1, z2, xb0, xb1, xb2,
):
    core = core_ref[0]
    other = 1 - core
    edges = esrc_ref.shape[1]
    atoms, half = fo_ref.shape

    for q, (own, oth) in enumerate(
        zip((fo_ref, ho0_ref, ho1_ref, ho2_ref, ho3_ref), (fx_ref, hx0_ref, hx1_ref, hx2_ref, hx3_ref))
    ):
        rows[core, q * atoms : (q + 1) * atoms, :] = own[...]
        rows[other, q * atoms : (q + 1) * atoms, :] = oth[...]

    source_rows = lax.broadcasted_iota(jnp.int32, (5 * atoms, edges), 0)
    onehot = (esrc_ref[...] == source_rows).astype(BF16)

    rot_count = rot_ref.shape[1]
    picks = (erot_ref[...] == lax.broadcasted_iota(jnp.int32, (rot_count, edges), 0)).astype(BF16)
    rot = rot_ref[...]
    rot_hi = rot.astype(BF16)
    rot_lo = (rot - rot_hi.astype(F32)).astype(BF16)
    packed[...] = dot(rot_hi, picks, 1, 0) + dot(rot_lo, picks, 1, 0)
    for blk in range(edges // 128):
        lanes = slice(blk * 128, (blk + 1) * 128)
        weight = jnp.broadcast_to(ew_ref[:, lanes], (8, 128))
        for slot, entry in SLOTS.values():
            value = jnp.broadcast_to(packed[entry : entry + 1, lanes], (8, 128))
            frames[blk, slot] = value
            wframes[blk, slot] = value * weight

    step = 640

    def gather(i, _):
        h = i // (half // step)
        n = i % (half // step)
        got = dot(rows[h, :, pl.ds(pl.multiple_of(n * step, 128), step)], onehot, 0, 0)
        at = pl.multiple_of(i * step, 8)
        for blk in range(edges // 128):
            nat[blk, pl.ds(at, step), :] = got[:, blk * 128 : (blk + 1) * 128]
        return 0

    lax.fori_loop(0, 2 * half // step, gather, 0)

    groups = 2 * half // 400

    def rotate_in(i, _):
        blk = i // groups
        g = i % groups
        for p in range(2):
            nb = blk * 2 + p
            for l in range(LMAX + 1):
                xs = [nat[blk, pl.ds(g * 400 + p * 25 + l * l + n, 8, stride=50), :] for n in range(2 * l + 1)]
                for m in range(-min(l, MMAX), min(l, MMAX) + 1):
                    acc = frames[blk, SLOTS[(l, m, 0)][0]] * xs[0]
                    for n in range(1, 2 * l + 1):
                        acc = acc + frames[blk, SLOTS[(l, m, n)][0]] * xs[n]
                    if m == 0:
                        z0[nb, pl.ds(g * 40 + l, 8, stride=5), :] = acc
                    else:
                        side = nb if m > 0 else nb + 4
                        if abs(m) == 1:
                            z1[side, pl.ds(g * 32 + l - 1, 8, stride=4), :] = acc
                        else:
                            z2[side, pl.ds(g * 24 + l - 2, 8, stride=3), :] = acc
        return 0

    lax.fori_loop(0, groups * (edges // 128), rotate_in, 0)

    for nb in range(4):
        xb0[:, nb * 128 : (nb + 1) * 128] = z0[nb].astype(BF16)
    for nb in range(8):
        xb1[:, nb * 128 : (nb + 1) * 128] = z1[nb].astype(BF16)
        xb2[:, nb * 128 : (nb + 1) * 128] = z2[nb].astype(BF16)

    def mix_zero(t, _):
        at = pl.multiple_of(t * 128, 128)
        y = dot(mix0_ref[:, pl.ds(at, 128)], xb0[...], 0, 0)
        for nb in range(4):
            z0[nb, pl.ds(at, 128), :] = y[:, nb * 128 : (nb + 1) * 128]
        return 0

    lax.fori_loop(0, mix0_ref.shape[1] // 128, mix_zero, 0)

    def mix_pair(mix_ref, xb, z):
        def tile(t, _):
            at = pl.multiple_of(t * 128, 128)
            a = dot(mix_ref[0, :, pl.ds(at, 128)], xb[...], 0, 0)
            b = dot(mix_ref[1, :, pl.ds(at, 128)], xb[...], 0, 0)
            for nb in range(4):
                lo = slice(nb * 128, (nb + 1) * 128)
                hi = slice(512 + nb * 128, 512 + (nb + 1) * 128)
                z[nb, pl.ds(at, 128), :] = a[:, lo] - b[:, hi]
                z[nb + 4, pl.ds(at, 128), :] = a[:, hi] + b[:, lo]
            return 0

        lax.fori_loop(0, mix_ref.shape[2] // 128, tile, 0)

    mix_pair(mix1_ref, xb1, z1)
    mix_pair(mix2_ref, xb2, z2)

    def rotate_out(i, _):
        blk = i // groups
        g = i % groups
        for p in range(2):
            nb = blk * 2 + p
            for l in range(LMAX + 1):
                ms = range(-min(l, MMAX), min(l, MMAX) + 1)
                ys = {}
                for m in ms:
                    side = nb if m >= 0 else nb + 4
                    if m == 0:
                        ys[m] = z0[nb, pl.ds(g * 40 + l, 8, stride=5), :]
                    elif abs(m) == 1:
                        ys[m] = z1[side, pl.ds(g * 32 + l - 1, 8, stride=4), :]
                    else:
                        ys[m] = z2[side, pl.ds(g * 24 + l - 2, 8, stride=3), :]
                for n in range(2 * l + 1):
                    acc = None
                    for m in ms:
                        term = wframes[blk, SLOTS[(l, m, n)][0]] * ys[m]
                        acc = term if acc is None else acc + term
                    nat[blk, pl.ds(g * 400 + p * 25 + l * l + n, 8, stride=50), :] = acc
        return 0

    lax.fori_loop(0, groups * (edges // 128), rotate_out, 0)

    scatter = (edst_ref[...] == lax.broadcasted_iota(jnp.int32, (atoms, edges), 0)).astype(BF16)

    def aggregate(i, _):
        at = pl.multiple_of(i * step, 128)
        msgs = jnp.concatenate(
            [nat[blk, pl.ds(at, step), :].astype(BF16) for blk in range(edges // 128)], axis=1
        )
        out_ref[:, pl.ds(at, step)] = dot(scatter, msgs, 1, 1).astype(BF16)
        return 0

    lax.fori_loop(0, 2 * half // step, aggregate, 0)


def messages(core, esrc, edst, erot, ew, rot_table, mixes, own, oth):
    edges = esrc.shape[-1]
    atoms, half = own[0].shape
    row = lambda a: a.reshape(1, -1)
    vmem = pl.BlockSpec(memory_space=pltpu.VMEM)
    return pl.pallas_call(
        message_kernel,
        out_shape=jax.ShapeDtypeStruct((atoms, 2 * half), BF16),
        in_specs=[pl.BlockSpec(memory_space=pltpu.SMEM)] + [vmem] * 18,
        out_specs=vmem,
        scratch_shapes=[
            pltpu.VMEM((2, 5 * atoms, half), BF16),
            pltpu.VMEM((edges // 128, 2 * half, 128), F32),
            pltpu.VMEM((edges // 128, len(SLOTS), 8, 128), F32),
            pltpu.VMEM((edges // 128, len(SLOTS), 8, 128), F32),
            pltpu.VMEM((rot_table.shape[0], edges), F32),
            pltpu.VMEM((4, 640, 128), F32),
            pltpu.VMEM((8, 512, 128), F32),
            pltpu.VMEM((8, 384, 128), F32),
            pltpu.VMEM((640, 512), BF16),
            pltpu.VMEM((512, 1024), BF16),
            pltpu.VMEM((384, 1024), BF16),
        ],
        compiler_params=pltpu.CompilerParams(vmem_limit_bytes=36 * 1024 * 1024),
        cost_estimate=pl.CostEstimate(flops=5_000_000_000, bytes_accessed=6_000_000, transcendentals=0),
        name="messages",
    )(core, row(esrc), row(edst), row(erot), row(ew), rot_table, *mixes, *own, *oth)


def head_kernel(
    core_ref, orbitals_ref, species_ref, fo_ref, fx_ref, mine_ref, recv_ref, weight_ref, target_ref,
    load_ref, loss_ref, keep_ref, send_ref,
    feats, upd,
):
    core = core_ref[0]
    atoms, half = fo_ref.shape
    feats[core] = fo_ref[...]
    feats[1 - core] = fx_ref[...]
    for h in range(2):
        cols = slice(h * half, (h + 1) * half)
        total = mine_ref[:, cols].astype(F32) + recv_ref[:, cols].astype(F32)
        upd[:, cols] = (feats[h].astype(F32) + BRANCH * total).astype(BF16)
    blocks = dot(upd[...], weight_ref[...], 1, 0)
    width = blocks.shape[1]
    species = species_ref[...]
    norb = jnp.zeros_like(species)
    for s in range(orbitals_ref.shape[0]):
        norb = jnp.where(species == s, orbitals_ref[s], norb)
    cols = core * width + lax.broadcasted_iota(jnp.int32, (atoms, width), 1)
    valid = ((cols // (2 * ORB)) < norb) & (((cols // 2) % ORB) < norb)
    error = jnp.where(valid, blocks - target_ref[...], 0.0)
    divisor = norb.astype(F32)
    loss_ref[...] = jnp.sum(error * error, axis=1, keepdims=True) / divisor
    dblk = (2.0 * error / divisor).astype(BF16)
    parts = load_ref.shape[0]
    share = 2 * half // parts
    for g in range(parts):
        where = (g % 2) * (parts // 2) + g // 2
        load_ref[where, :, :width] = dblk
        load_ref[where, :, width : width + share] = upd[:, g * share : (g + 1) * share]
        load_ref[where, :, width + share :] = jnp.zeros((atoms, width - share), BF16)
    keep_ref[...] = dot(dblk, weight_ref[pl.ds(pl.multiple_of(core * half, 128), half), :], 1, 1)
    send_ref[...] = dot(dblk, weight_ref[pl.ds(pl.multiple_of((1 - core) * half, 128), half), :], 1, 1).astype(BF16)


def head(core, orbitals, species, f_own, f_oth, mine, recv, weight, target, parts):
    atoms, half = f_own.shape
    smem = pl.BlockSpec(memory_space=pltpu.SMEM)
    vmem = pl.BlockSpec(memory_space=pltpu.VMEM)
    return pl.pallas_call(
        head_kernel,
        out_shape=(
            jax.ShapeDtypeStruct((parts, atoms, 2 * target.shape[1]), BF16),
            jax.ShapeDtypeStruct((atoms, 1), F32),
            jax.ShapeDtypeStruct((atoms, half), F32),
            jax.ShapeDtypeStruct((atoms, half), BF16),
        ),
        in_specs=[smem, smem] + [vmem] * 7,
        out_specs=(vmem,) * 4,
        scratch_shapes=[pltpu.VMEM((2, atoms, half), BF16), pltpu.VMEM((atoms, 2 * half), BF16)],
        compiler_params=pltpu.CompilerParams(vmem_limit_bytes=32 * 1024 * 1024),
        cost_estimate=pl.CostEstimate(flops=300_000_000, bytes_accessed=6_000_000, transcendentals=0),
        name="head",
    )(core, orbitals, species.reshape(-1, 1), f_own, f_oth, mine, recv, weight, target)


def leaving_kernel(sends_ref, feats_ref, *outs):
    atoms = feats_ref.shape[0]
    places = lax.broadcasted_iota(jnp.int32, (atoms, atoms), 0)
    picks = jnp.concatenate(
        [(sends_ref[q : q + 1, :] == places).astype(F32) for q in range(len(outs))], axis=1
    ).astype(BF16)
    rows = dot(picks, feats_ref[...], 0, 0).astype(BF16)
    for q, out in enumerate(outs):
        out[...] = rows[q * atoms : (q + 1) * atoms, :]


def leaving_rows(send_rows, features):
    vmem = pl.BlockSpec(memory_space=pltpu.VMEM)
    return pl.pallas_call(
        leaving_kernel,
        out_shape=(jax.ShapeDtypeStruct(features.shape, BF16),) * len(OFFSETS),
        in_specs=[vmem, vmem],
        out_specs=(vmem,) * len(OFFSETS),
        compiler_params=pltpu.CompilerParams(vmem_limit_bytes=24 * 1024 * 1024),
        name="leaving",
    )(send_rows, features)


def partial_kernel(got_ref, out_ref):
    width = got_ref.shape[1] // 2
    full = dot(got_ref[:, width:], got_ref[:, :width], 0, 0)
    out_ref[...] = full[: out_ref.shape[0]].astype(BF16)


def partial_grad(got, share):
    vmem = pl.BlockSpec(memory_space=pltpu.VMEM)
    return pl.pallas_call(
        partial_kernel,
        out_shape=jax.ShapeDtypeStruct((share, got.shape[1] // 2), BF16),
        in_specs=[vmem],
        out_specs=vmem,
        compiler_params=pltpu.CompilerParams(vmem_limit_bytes=24 * 1024 * 1024),
        name="partial_grad",
    )(got)


def shift(x, axis, by):
    count = lax.axis_size(axis)
    return lax.ppermute(x, axis, [(i, (i + by) % count) for i in range(count)])


def ring_blocks(x, axis):
    half = x.shape[0] // 2
    behind = shift(x, axis, 1)
    ahead = shift(x, axis, -1)
    return [x, behind, shift(behind[:half], axis, 1), shift(ahead[half:], axis, -1), ahead]


def assemble_kernel(place_ref, *refs):
    blocks, out_ref, sems = refs[:-2], refs[-2], refs[-1]
    y, x = place_ref[0], place_ref[1]
    rows = out_ref.shape[0] // 16
    copies = []
    for path in range(2):
        own, behind, far_lo, far_hi, ahead = blocks[5 * path : 5 * path + 5]
        for late in range(4):
            for early in range(4):
                if late == 2:
                    ref, at = (far_lo, early) if early < 2 else (far_hi, early - 2)
                else:
                    ref, at = {0: own, 1: behind, 3: ahead}[late], early
                dy, dx = (late, early) if path == 0 else (early, late)
                spot = lax.rem(y + 4 - dy, 4) * 4 + lax.rem(x + 4 - dx, 4)
                copies.append(
                    pltpu.make_async_copy(
                        ref.at[pl.ds(at * rows, rows), :],
                        out_ref.at[pl.ds(pl.multiple_of(spot * rows, 16), rows), pl.ds(path * 128, 128)],
                        sems.at[len(copies)],
                    )
                )
    for copy in copies:
        copy.start()
    for copy in copies:
        copy.wait()


def assemble(place, blocks):
    rows = 4 * blocks[0].shape[0]
    hbm = pl.BlockSpec(memory_space=pl.ANY)
    return pl.pallas_call(
        assemble_kernel,
        out_shape=jax.ShapeDtypeStruct((rows, 256), BF16),
        in_specs=[pl.BlockSpec(memory_space=pltpu.SMEM)]
        + [pl.BlockSpec(memory_space=pltpu.VMEM)] * len(blocks),
        out_specs=hbm,
        scratch_shapes=[pltpu.SemaphoreType.DMA((32,))],
        compiler_params=pltpu.CompilerParams(vmem_limit_bytes=16 * 1024 * 1024),
        name="assemble",
    )(place, *blocks)


def body(
    features, send_rows, edge_source, edge_dest, edge_rot, edge_weight, rot_table,
    mix_zero, mix_one, mix_two, atom_species, species_orbitals, head_weight, target_blocks,
):
    core = lax.axis_index("chan").astype(jnp.int32).reshape(1)
    f_oth = shift(features, "chan", 1)
    halo = [shift(rows, ATOMS, off) for rows, off in zip(leaving_rows(send_rows, features), OFFSETS)]
    halo_oth = [shift(h, "chan", 1) for h in halo]
    mine = messages(
        core, edge_source, edge_dest, edge_rot, edge_weight, rot_table.T,
        (mix_zero, mix_one, mix_two), [features] + halo, [f_oth] + halo_oth,
    )
    recv = shift(mine, "chan", 1)
    parts = lax.axis_size(GROUP)
    load, loss, keep, send = head(
        core, species_orbitals, atom_species, features, f_oth, mine, recv, head_weight, target_blocks, parts
    )
    got = lax.all_to_all(load, GROUP, split_axis=0, concat_axis=0, tiled=True)
    atom_loss = loss[:, 0] + shift(loss[:, 0], "chan", 1)
    grad_features = keep + shift(send, "chan", 1).astype(F32)
    share = 2 * features.shape[1] // parts
    part = partial_grad(got.reshape(-1, got.shape[2]), share)
    near = shift(part, "zh", 1).astype(F32) + shift(part, "zh", -1).astype(F32)
    total = (part.astype(F32) + shift(part, "zh", 2).astype(F32) + near).astype(BF16)
    twin = shift(total, "zl", 1)
    low = lax.axis_index("zl") == 0
    pair = jnp.concatenate([jnp.where(low, total, twin), jnp.where(low, twin, total)], axis=0)

    def gather_first(x, axis):
        own, behind, far_lo, far_hi, ahead = ring_blocks(x, axis)
        return jnp.concatenate([own, behind, far_lo, far_hi, ahead], axis=0)

    left = gather_first(pair[:, :128], "x")
    right = gather_first(pair[:, 128:], "y")
    place = jnp.stack([lax.axis_index("y"), lax.axis_index("x")]).astype(jnp.int32)
    grad_head = assemble(place, ring_blocks(left, "y") + ring_blocks(right, "x"))
    return (atom_loss, grad_head, grad_features)


def solution(mesh):
    fine = Mesh(mesh.devices.reshape(4, 2, 4, 4, 2), ("zh", "zl", "y", "x", "chan"))
    both = ATOMS + ("chan",)
    return jax.shard_map(
        body,
        mesh=fine,
        in_specs=(
            P(ATOMS, "chan"), P(ATOMS, None), P(both), P(both), P(both), P(both),
            P(), P(), P(), P(), P(ATOMS), P(), P(None, "chan"), P(ATOMS, "chan"),
        ),
        out_specs=(P(ATOMS), P(None, "chan"), P(ATOMS, "chan")),
        check_vma=False,
    )
```

```python
import functools
import jax
import jax.numpy as jnp
import numpy as np
from jax import lax
from jax.experimental import pallas as pl
from jax.experimental.pallas import tpu as pltpu
from jax.sharding import Mesh, PartitionSpec as P

ORB = 16
LMAX = 4
MMAX = 2
OFFSETS = (1, -1, 2, -2)
BRANCH = 0.125
GROUP = ("zl", "y", "x")
ATOMS = ("zh", "zl", "y", "x")
F32 = jnp.float32
BF16 = jnp.bfloat16


def frame_entries():
    slots = {}
    start = 0
    for l in range(LMAX + 1):
        width = 2 * l + 1
        for m in range(-min(l, MMAX), min(l, MMAX) + 1):
            for n in range(width):
                slots[(l, m, n)] = (len(slots), start + (l + m) * width + n)
        start += width * width
    return slots


SLOTS = frame_entries()


def dot(a, b, ca, cb):
    return lax.dot_general(a, b, (((ca,), (cb,)), ((), ())), preferred_element_type=F32)


def message_kernel(
    core_ref, esrc_hbm, edst_hbm, erot_hbm, ew_hbm, rot_hbm,
    mix0_hbm, mix1_hbm, mix2_hbm,
    fo_ref, ho0_ref, ho1_ref, ho2_ref, ho3_ref,
    fx_ref, hx0_ref, hx1_ref, hx2_ref, hx3_ref,
    out_ref,
    rows, nat, frames, wframes, packed, z0, z1, z2, xb0, xb1, xb2,
    esrc_ref, edst_ref, erot_ref, ew_ref, rot_ref, mix0_ref, mix1_ref, mix2_ref, sems,
):
    core = core_ref[0]
    other = 1 - core
    edges = esrc_ref.shape[1]
    atoms, half = fo_ref.shape

    copies = [
        pltpu.make_async_copy(src, dst, sems.at[i])
        for i, (src, dst) in enumerate(
            (
                (erot_hbm, erot_ref), (ew_hbm, ew_ref), (rot_hbm, rot_ref), (esrc_hbm, esrc_ref),
                (edst_hbm, edst_ref), (mix0_hbm, mix0_ref), (mix1_hbm, mix1_ref), (mix2_hbm, mix2_ref),
            )
        )
    ]
    moves = []
    for q, (own, oth) in enumerate(
        zip((fo_ref, ho0_ref, ho1_ref, ho2_ref, ho3_ref), (fx_ref, hx0_ref, hx1_ref, hx2_ref, hx3_ref))
    ):
        at = pl.ds(q * atoms, atoms)
        moves.append(pltpu.make_async_copy(own, rows.at[core, at, :], sems.at[8 + 2 * q]))
        moves.append(pltpu.make_async_copy(oth, rows.at[other, at, :], sems.at[9 + 2 * q]))
    for copy in copies[:5] + moves + copies[5:]:
        copy.start()
    for copy in copies[:5]:
        copy.wait()

    source_rows = lax.broadcasted_iota(jnp.int32, (5 * atoms, edges), 0)
    onehot = (esrc_ref[...] == source_rows).astype(BF16)

    rot_count = rot_ref.shape[1]
    picks = (erot_ref[...] == lax.broadcasted_iota(jnp.int32, (rot_count, edges), 0)).astype(BF16)
    rot = rot_ref[...]
    rot_hi = rot.astype(BF16)
    rot_lo = (rot - rot_hi.astype(F32)).astype(BF16)
    packed[...] = dot(rot_hi, picks, 1, 0) + dot(rot_lo, picks, 1, 0)
    for blk in range(edges // 128):
        lanes = slice(blk * 128, (blk + 1) * 128)
        weight = jnp.broadcast_to(ew_ref[:, lanes], (8, 128))
        for slot, entry in SLOTS.values():
            value = jnp.broadcast_to(packed[entry : entry + 1, lanes], (8, 128))
            frames[blk, slot] = value
            wframes[blk, slot] = value * weight

    step = 640

    def gather(i, _):
        h = i // (half // step)
        n = i % (half // step)
        got = dot(rows[h, :, pl.ds(pl.multiple_of(n * step, 128), step)], onehot, 0, 0)
        at = pl.multiple_of(i * step, 8)
        for blk in range(edges // 128):
            nat[blk, pl.ds(at, step), :] = got[:, blk * 128 : (blk + 1) * 128]
        return 0

    for move in moves:
        move.wait()
    lax.fori_loop(0, 2 * half // step, gather, 0)

    groups = 2 * half // 400

    def rotate_in(i, _):
        blk = i // groups
        g = i % groups
        for p in range(2):
            nb = blk * 2 + p
            for l in range(LMAX + 1):
                xs = [nat[blk, pl.ds(g * 400 + p * 25 + l * l + n, 8, stride=50), :] for n in range(2 * l + 1)]
                for m in range(-min(l, MMAX), min(l, MMAX) + 1):
                    acc = frames[blk, SLOTS[(l, m, 0)][0]] * xs[0]
                    for n in range(1, 2 * l + 1):
                        acc = acc + frames[blk, SLOTS[(l, m, n)][0]] * xs[n]
                    if m == 0:
                        z0[nb, pl.ds(g * 40 + l, 8, stride=5), :] = acc
                    else:
                        side = nb if m > 0 else nb + 4
                        if abs(m) == 1:
                            z1[side, pl.ds(g * 32 + l - 1, 8, stride=4), :] = acc
                        else:
                            z2[side, pl.ds(g * 24 + l - 2, 8, stride=3), :] = acc
        return 0

    lax.fori_loop(0, groups * (edges // 128), rotate_in, 0)

    for nb in range(4):
        xb0[:, nb * 128 : (nb + 1) * 128] = z0[nb].astype(BF16)
    for nb in range(8):
        xb1[:, nb * 128 : (nb + 1) * 128] = z1[nb].astype(BF16)
        xb2[:, nb * 128 : (nb + 1) * 128] = z2[nb].astype(BF16)

    def mix_zero(t, _):
        at = pl.multiple_of(t * 128, 128)
        y = dot(mix0_ref[:, pl.ds(at, 128)], xb0[...], 0, 0)
        for nb in range(4):
            z0[nb, pl.ds(at, 128), :] = y[:, nb * 128 : (nb + 1) * 128]
        return 0

    for copy in copies[5:]:
        copy.wait()
    lax.fori_loop(0, mix0_ref.shape[1] // 128, mix_zero, 0)

    def mix_pair(mix_ref, xb, z):
        def tile(t, _):
            at = pl.multiple_of(t * 128, 128)
            a = dot(mix_ref[0, :, pl.ds(at, 128)], xb[...], 0, 0)
            b = dot(mix_ref[1, :, pl.ds(at, 128)], xb[...], 0, 0)
            for nb in range(4):
                lo = slice(nb * 128, (nb + 1) * 128)
                hi = slice(512 + nb * 128, 512 + (nb + 1) * 128)
                z[nb, pl.ds(at, 128), :] = a[:, lo] - b[:, hi]
                z[nb + 4, pl.ds(at, 128), :] = a[:, hi] + b[:, lo]
            return 0

        lax.fori_loop(0, mix_ref.shape[2] // 128, tile, 0)

    mix_pair(mix1_ref, xb1, z1)
    mix_pair(mix2_ref, xb2, z2)

    def rotate_out(i, _):
        blk = i // groups
        g = i % groups
        for p in range(2):
            nb = blk * 2 + p
            for l in range(LMAX + 1):
                ms = range(-min(l, MMAX), min(l, MMAX) + 1)
                ys = {}
                for m in ms:
                    side = nb if m >= 0 else nb + 4
                    if m == 0:
                        ys[m] = z0[nb, pl.ds(g * 40 + l, 8, stride=5), :]
                    elif abs(m) == 1:
                        ys[m] = z1[side, pl.ds(g * 32 + l - 1, 8, stride=4), :]
                    else:
                        ys[m] = z2[side, pl.ds(g * 24 + l - 2, 8, stride=3), :]
                for n in range(2 * l + 1):
                    acc = None
                    for m in ms:
                        term = wframes[blk, SLOTS[(l, m, n)][0]] * ys[m]
                        acc = term if acc is None else acc + term
                    nat[blk, pl.ds(g * 400 + p * 25 + l * l + n, 8, stride=50), :] = acc
        return 0

    lax.fori_loop(0, groups * (edges // 128), rotate_out, 0)

    scatter = (edst_ref[...] == lax.broadcasted_iota(jnp.int32, (atoms, edges), 0)).astype(BF16)

    def aggregate(i, _):
        at = pl.multiple_of(i * step, 128)
        msgs = jnp.concatenate(
            [nat[blk, pl.ds(at, step), :].astype(BF16) for blk in range(edges // 128)], axis=1
        )
        out_ref[:, pl.ds(at, step)] = dot(scatter, msgs, 1, 1).astype(BF16)
        return 0

    lax.fori_loop(0, 2 * half // step, aggregate, 0)


def messages(core, esrc, edst, erot, ew, rot_table, mixes, own, oth):
    edges = esrc.shape[-1]
    atoms, half = own[0].shape
    row = lambda a: a.reshape(1, -1)
    vmem = pl.BlockSpec(memory_space=pltpu.VMEM)
    return pl.pallas_call(
        message_kernel,
        out_shape=jax.ShapeDtypeStruct((atoms, 2 * half), BF16),
        in_specs=[pl.BlockSpec(memory_space=pltpu.SMEM)] + [pl.BlockSpec(memory_space=pltpu.HBM)] * 18,
        out_specs=vmem,
        scratch_shapes=[
            pltpu.VMEM((2, 5 * atoms, half), BF16),
            pltpu.VMEM((edges // 128, 2 * half, 128), F32),
            pltpu.VMEM((edges // 128, len(SLOTS), 8, 128), F32),
            pltpu.VMEM((edges // 128, len(SLOTS), 8, 128), F32),
            pltpu.VMEM((rot_table.shape[0], edges), F32),
            pltpu.VMEM((4, 640, 128), F32),
            pltpu.VMEM((8, 512, 128), F32),
            pltpu.VMEM((8, 384, 128), F32),
            pltpu.VMEM((640, 512), BF16),
            pltpu.VMEM((512, 1024), BF16),
            pltpu.VMEM((384, 1024), BF16),
        ]
        + [pltpu.VMEM((1, edges), jnp.int32)] * 3
        + [pltpu.VMEM((1, edges), F32), pltpu.VMEM(rot_table.shape, F32)]
        + [pltpu.VMEM(mix.shape, BF16) for mix in mixes]
        + [pltpu.SemaphoreType.DMA((18,))],
        compiler_params=pltpu.CompilerParams(vmem_limit_bytes=54 * 1024 * 1024),
        cost_estimate=pl.CostEstimate(flops=5_000_000_000, bytes_accessed=6_000_000, transcendentals=0),
        name="messages",
    )(core, row(esrc), row(edst), row(erot), row(ew), rot_table, *mixes, *own, *oth)


def head_kernel(
    core_ref, orbitals_ref, species_ref, fo_ref, fx_ref, mine_ref, recv_ref, weight_ref, target_ref,
    load_ref, loss_ref, keep_ref, send_ref,
    feats, upd,
):
    core = core_ref[0]
    atoms, half = fo_ref.shape
    feats[core] = fo_ref[...]
    feats[1 - core] = fx_ref[...]
    for h in range(2):
        cols = slice(h * half, (h + 1) * half)
        total = mine_ref[:, cols].astype(F32) + recv_ref[:, cols].astype(F32)
        upd[:, cols] = (feats[h].astype(F32) + BRANCH * total).astype(BF16)
    blocks = dot(upd[...], weight_ref[...], 1, 0)
    width = blocks.shape[1]
    species = species_ref[...]
    norb = jnp.zeros_like(species)
    for s in range(orbitals_ref.shape[0]):
        norb = jnp.where(species == s, orbitals_ref[s], norb)
    cols = core * width + lax.broadcasted_iota(jnp.int32, (atoms, width), 1)
    valid = ((cols // (2 * ORB)) < norb) & (((cols // 2) % ORB) < norb)
    error = jnp.where(valid, blocks - target_ref[...], 0.0)
    divisor = norb.astype(F32)
    loss_ref[...] = jnp.sum(error * error, axis=1, keepdims=True) / divisor
    dblk = (2.0 * error / divisor).astype(BF16)
    parts = load_ref.shape[0]
    share = 2 * half // parts
    for g in range(parts):
        where = (g % 2) * (parts // 2) + g // 2
        load_ref[where, :, :width] = dblk
        load_ref[where, :, width : width + share] = upd[:, g * share : (g + 1) * share]
        load_ref[where, :, width + share :] = jnp.zeros((atoms, width - share), BF16)
    keep_ref[...] = dot(dblk, weight_ref[pl.ds(pl.multiple_of(core * half, 128), half), :], 1, 1)
    send_ref[...] = dot(dblk, weight_ref[pl.ds(pl.multiple_of((1 - core) * half, 128), half), :], 1, 1).astype(BF16)


def head(core, orbitals, species, f_own, f_oth, mine, recv, weight, target, parts):
    atoms, half = f_own.shape
    smem = pl.BlockSpec(memory_space=pltpu.SMEM)
    vmem = pl.BlockSpec(memory_space=pltpu.VMEM)
    return pl.pallas_call(
        head_kernel,
        out_shape=(
            jax.ShapeDtypeStruct((parts, atoms, 2 * target.shape[1]), BF16),
            jax.ShapeDtypeStruct((atoms, 1), F32),
            jax.ShapeDtypeStruct((atoms, half), F32),
            jax.ShapeDtypeStruct((atoms, half), BF16),
        ),
        in_specs=[smem, smem] + [vmem] * 7,
        out_specs=(vmem,) * 4,
        scratch_shapes=[pltpu.VMEM((2, atoms, half), BF16), pltpu.VMEM((atoms, 2 * half), BF16)],
        compiler_params=pltpu.CompilerParams(vmem_limit_bytes=32 * 1024 * 1024),
        cost_estimate=pl.CostEstimate(flops=300_000_000, bytes_accessed=6_000_000, transcendentals=0),
        name="head",
    )(core, orbitals, species.reshape(-1, 1), f_own, f_oth, mine, recv, weight, target)


def leaving_kernel(sends_ref, feats_ref, *outs):
    atoms = feats_ref.shape[0]
    places = lax.broadcasted_iota(jnp.int32, (atoms, atoms), 0)
    picks = jnp.concatenate(
        [(sends_ref[q : q + 1, :] == places).astype(F32) for q in range(len(outs))], axis=1
    ).astype(BF16)
    rows = dot(picks, feats_ref[...], 0, 0).astype(BF16)
    for q, out in enumerate(outs):
        out[...] = rows[q * atoms : (q + 1) * atoms, :]


def leaving_rows(send_rows, features):
    vmem = pl.BlockSpec(memory_space=pltpu.VMEM)
    return pl.pallas_call(
        leaving_kernel,
        out_shape=(jax.ShapeDtypeStruct(features.shape, BF16),) * len(OFFSETS),
        in_specs=[vmem, vmem],
        out_specs=(vmem,) * len(OFFSETS),
        compiler_params=pltpu.CompilerParams(vmem_limit_bytes=24 * 1024 * 1024),
        name="leaving",
    )(send_rows, features)


def partial_kernel(got_ref, out_ref):
    width = got_ref.shape[1] // 2
    full = dot(got_ref[:, width:], got_ref[:, :width], 0, 0)
    out_ref[...] = full[: out_ref.shape[0]].astype(BF16)


def partial_grad(got, share):
    vmem = pl.BlockSpec(memory_space=pltpu.VMEM)
    return pl.pallas_call(
        partial_kernel,
        out_shape=jax.ShapeDtypeStruct((share, got.shape[1] // 2), BF16),
        in_specs=[vmem],
        out_specs=vmem,
        compiler_params=pltpu.CompilerParams(vmem_limit_bytes=24 * 1024 * 1024),
        name="partial_grad",
    )(got)


def shift(x, axis, by):
    count = lax.axis_size(axis)
    return lax.ppermute(x, axis, [(i, (i + by) % count) for i in range(count)])


def plane_shift(x, early, by):
    pairs = []
    for y in range(4):
        for x_at in range(4):
            for c in range(2):
                along_x = (c == 0) == early
                to = (y, (x_at + by) % 4) if along_x else ((y + by) % 4, x_at)
                pairs.append(((y * 4 + x_at) * 2 + c, (to[0] * 4 + to[1]) * 2 + c))
    return lax.ppermute(x, ("y", "x", "chan"), pairs)


def assemble_kernel(place_ref, own, behind, far_lo, far_hi, ahead, out_ref, sems):
    y, x, core = place_ref[0], place_ref[1], place_ref[2]
    rows = out_ref.shape[0] // 16
    copies = []
    for late in range(4):
        for early in range(4):
            if late == 2:
                ref, at = (far_lo, early) if early < 2 else (far_hi, early - 2)
            else:
                ref, at = {0: own, 1: behind, 3: ahead}[late], early
            dy = late + core * (early - late)
            dx = early + core * (late - early)
            spot = lax.rem(y + 4 - dy, 4) * 4 + lax.rem(x + 4 - dx, 4)
            copies.append(
                pltpu.make_async_copy(
                    ref.at[pl.ds(at * rows, rows), :],
                    out_ref.at[pl.ds(pl.multiple_of(spot * rows, 16), rows), :],
                    sems.at[len(copies)],
                )
            )
    for copy in copies:
        copy.start()
    for copy in copies:
        copy.wait()


def assemble(place, blocks):
    rows, width = blocks[0].shape
    return pl.pallas_call(
        assemble_kernel,
        out_shape=jax.ShapeDtypeStruct((4 * rows, width), BF16),
        in_specs=[pl.BlockSpec(memory_space=pltpu.SMEM)]
        + [pl.BlockSpec(memory_space=pltpu.VMEM)] * len(blocks),
        out_specs=pl.BlockSpec(memory_space=pl.ANY),
        scratch_shapes=[pltpu.SemaphoreType.DMA((16,))],
        compiler_params=pltpu.CompilerParams(vmem_limit_bytes=16 * 1024 * 1024),
        name="assemble",
    )(place, *blocks)


def body(
    features, send_rows, edge_source, edge_dest, edge_rot, edge_weight, rot_table,
    mix_zero, mix_one, mix_two, atom_species, species_orbitals, head_weight, target_blocks,
):
    core = lax.axis_index("chan").astype(jnp.int32).reshape(1)
    f_oth = shift(features, "chan", 1)
    halo = [shift(rows, ATOMS, off) for rows, off in zip(leaving_rows(send_rows, features), OFFSETS)]
    halo_oth = [shift(h, "chan", 1) for h in halo]
    mine = messages(
        core, edge_source, edge_dest, edge_rot, edge_weight, rot_table.T,
        (mix_zero, mix_one, mix_two), [features] + halo, [f_oth] + halo_oth,
    )
    recv = shift(mine, "chan", 1)
    parts = lax.axis_size(GROUP)
    load, loss, keep, send = head(
        core, species_orbitals, atom_species, features, f_oth, mine, recv, head_weight, target_blocks, parts
    )
    got = lax.all_to_all(load, GROUP, split_axis=0, concat_axis=0, tiled=True)
    atom_loss = loss[:, 0] + shift(loss[:, 0], "chan", 1)
    grad_features = keep + shift(send, "chan", 1).astype(F32)
    share = 2 * features.shape[1] // parts
    part = partial_grad(got.reshape(-1, got.shape[2]), share)
    near = shift(part, "zh", 1).astype(F32) + shift(part, "zh", -1).astype(F32)
    total = (part.astype(F32) + shift(part, "zh", 2).astype(F32) + near).astype(BF16)
    twin = shift(total, "zl", 1)
    low = lax.axis_index("zl") == 0
    pair = jnp.concatenate([jnp.where(low, total, twin), jnp.where(low, twin, total)], axis=0)

    row = jnp.concatenate(
        [pair, plane_shift(pair, True, 1), plane_shift(pair, True, 2), plane_shift(pair, True, -1)], axis=0
    )
    half = row.shape[0] // 2
    behind = plane_shift(row, False, 1)
    ahead = plane_shift(row, False, -1)
    far = [plane_shift(behind[:half], False, 1), plane_shift(ahead[half:], False, -1)]
    place = jnp.stack([lax.axis_index(name) for name in ("y", "x", "chan")]).astype(jnp.int32)
    grad_head = assemble(place, [row, behind] + far + [ahead])
    return (atom_loss, grad_head, grad_features)


def solution(mesh):
    fine = Mesh(mesh.devices.reshape(4, 2, 4, 4, 2), ("zh", "zl", "y", "x", "chan"))
    both = ATOMS + ("chan",)
    return jax.shard_map(
        body,
        mesh=fine,
        in_specs=(
            P(ATOMS, "chan"), P(ATOMS, None), P(both), P(both), P(both), P(both),
            P(), P(), P(), P(), P(ATOMS), P(), P(None, "chan"), P(ATOMS, "chan"),
        ),
        out_specs=(P(ATOMS), P(None, "chan"), P(ATOMS, "chan")),
        check_vma=False,
    )
```

```python
import functools
import jax
import jax.numpy as jnp
import numpy as np
from jax import lax
from jax.experimental import pallas as pl
from jax.experimental.pallas import tpu as pltpu
from jax.sharding import Mesh, PartitionSpec as P

ORB = 16
LMAX = 4
MMAX = 2
OFFSETS = (1, -1, 2, -2)
HALO_ORDER = (1, 2, -1, -2)
BRANCH = 0.125
GROUP = ("zl", "y", "x")
ATOMS = ("zh", "zl", "y", "x")
F32 = jnp.float32
BF16 = jnp.bfloat16


def frame_entries():
    slots = {}
    start = 0
    for l in range(LMAX + 1):
        width = 2 * l + 1
        for m in range(-min(l, MMAX), min(l, MMAX) + 1):
            for n in range(width):
                slots[(l, m, n)] = (len(slots), start + (l + m) * width + n)
        start += width * width
    return slots


SLOTS = frame_entries()


def dot(a, b, ca, cb):
    return lax.dot_general(a, b, (((ca,), (cb,)), ((), ())), preferred_element_type=F32)


def message_kernel(
    core_ref, esrc_hbm, edst_hbm, erot_hbm, ew_hbm, rot_hbm,
    mix0_hbm, mix1_hbm, mix2_hbm,
    fo_ref, ho0_ref, ho1_ref, ho2_ref, ho3_ref,
    fx_ref, hx0_ref, hx1_ref, hx2_ref, hx3_ref,
    out_ref,
    rows, nat, frames, wframes, packed, z0, z1, z2, xb0, xb1, xb2,
    esrc_ref, edst_ref, erot_ref, ew_ref, rot_ref, mix0_in, mix1_in, mix2_in, mix0_ref, mix1_ref, mix2_ref, sems,
):
    core = core_ref[0]
    other = 1 - core
    edges = esrc_ref.shape[1]
    atoms, half = fo_ref.shape

    copies = [
        pltpu.make_async_copy(src, dst, sems.at[i])
        for i, (src, dst) in enumerate(
            (
                (erot_hbm, erot_ref), (ew_hbm, ew_ref), (rot_hbm, rot_ref), (esrc_hbm, esrc_ref),
                (edst_hbm, edst_ref), (mix0_hbm, mix0_in), (mix1_hbm, mix1_in), (mix2_hbm, mix2_in),
            )
        )
    ]
    moves = []
    for q, (own, oth) in enumerate(
        zip((fo_ref, ho0_ref, ho1_ref, ho2_ref, ho3_ref), (fx_ref, hx0_ref, hx1_ref, hx2_ref, hx3_ref))
    ):
        at = pl.ds(0 if q == 0 else (1 + OFFSETS.index(HALO_ORDER[q - 1])) * atoms, atoms)
        moves.append(pltpu.make_async_copy(own, rows.at[core, at, :], sems.at[8 + 2 * q]))
        moves.append(pltpu.make_async_copy(oth, rows.at[other, at, :], sems.at[9 + 2 * q]))
    for copy in copies[:5] + moves + copies[5:]:
        copy.start()
    for copy in copies[:5]:
        copy.wait()

    source_rows = lax.broadcasted_iota(jnp.int32, (5 * atoms, edges), 0)
    onehot = (esrc_ref[...] == source_rows).astype(BF16)

    rot_count = rot_ref.shape[1]
    picks = (erot_ref[...] == lax.broadcasted_iota(jnp.int32, (rot_count, edges), 0)).astype(BF16)
    rot = rot_ref[...]
    rot_hi = rot.astype(BF16)
    rot_lo = (rot - rot_hi.astype(F32)).astype(BF16)
    packed[...] = dot(rot_hi, picks, 1, 0) + dot(rot_lo, picks, 1, 0)
    for blk in range(edges // 128):
        lanes = slice(blk * 128, (blk + 1) * 128)
        weight = jnp.broadcast_to(ew_ref[:, lanes], (8, 128))
        for slot, entry in SLOTS.values():
            value = jnp.broadcast_to(packed[entry : entry + 1, lanes], (8, 128))
            frames[blk, slot] = value
            wframes[blk, slot] = value * weight

    step = 640

    def gather(i, _):
        h = i // (half // step)
        n = i % (half // step)
        got = dot(rows[h, :, pl.ds(pl.multiple_of(n * step, 128), step)], onehot, 0, 0)
        at = pl.multiple_of(i * step, 8)
        for blk in range(edges // 128):
            nat[blk, pl.ds(at, step), :] = got[:, blk * 128 : (blk + 1) * 128]
        return 0

    for copy in copies[5:]:
        copy.wait()
    mix0_ref[...] = mix0_in[...].T
    for i in range(2):
        mix1_ref[i] = mix1_in[i].T
        mix2_ref[i] = mix2_in[i].T
    for move in moves:
        move.wait()
    lax.fori_loop(0, 2 * half // step, gather, 0)

    groups = 2 * half // 400

    def rotate_in(i, _):
        blk = i // groups
        g = i % groups
        for p in range(2):
            nb = blk * 2 + p
            for l in range(LMAX + 1):
                xs = [nat[blk, pl.ds(g * 400 + p * 25 + l * l + n, 8, stride=50), :] for n in range(2 * l + 1)]
                for m in range(-min(l, MMAX), min(l, MMAX) + 1):
                    acc = frames[blk, SLOTS[(l, m, 0)][0]] * xs[0]
                    for n in range(1, 2 * l + 1):
                        acc = acc + frames[blk, SLOTS[(l, m, n)][0]] * xs[n]
                    if m == 0:
                        z0[nb, pl.ds(g * 40 + l, 8, stride=5), :] = acc
                    else:
                        side = nb if m > 0 else nb + 4
                        if abs(m) == 1:
                            z1[side, pl.ds(g * 32 + l - 1, 8, stride=4), :] = acc
                        else:
                            z2[side, pl.ds(g * 24 + l - 2, 8, stride=3), :] = acc
        return 0

    lax.fori_loop(0, groups * (edges // 128), rotate_in, 0)

    for nb in range(4):
        xb0[:, nb * 128 : (nb + 1) * 128] = z0[nb].astype(BF16)
    for nb in range(8):
        xb1[:, nb * 128 : (nb + 1) * 128] = z1[nb].astype(BF16)
        xb2[:, nb * 128 : (nb + 1) * 128] = z2[nb].astype(BF16)

    def mix_zero(n, _):
        y = dot(mix0_ref[...], xb0[:, pl.ds(pl.multiple_of(n * 256, 256), 256)], 1, 0)
        z0[2 * n] = y[:, :128]
        z0[2 * n + 1] = y[:, 128:]
        return 0

    lax.fori_loop(0, 2, mix_zero, 0)

    def mix_pair(mix_ref, xb, z):
        def part(n, _):
            plus = xb[:, pl.ds(pl.multiple_of(n * 256, 256), 256)]
            minus = xb[:, pl.ds(pl.multiple_of(n * 256 + 512, 256), 256)]
            y = dot(mix_ref[0], plus, 1, 0) - dot(mix_ref[1], minus, 1, 0)
            z[2 * n] = y[:, :128]
            z[2 * n + 1] = y[:, 128:]
            y = dot(mix_ref[0], minus, 1, 0) + dot(mix_ref[1], plus, 1, 0)
            z[2 * n + 4] = y[:, :128]
            z[2 * n + 5] = y[:, 128:]
            return 0

        lax.fori_loop(0, 2, part, 0)

    mix_pair(mix1_ref, xb1, z1)
    mix_pair(mix2_ref, xb2, z2)

    def rotate_out(i, _):
        blk = i // groups
        g = i % groups
        for p in range(2):
            nb = blk * 2 + p
            for l in range(LMAX + 1):
                ms = range(-min(l, MMAX), min(l, MMAX) + 1)
                ys = {}
                for m in ms:
                    side = nb if m >= 0 else nb + 4
                    if m == 0:
                        ys[m] = z0[nb, pl.ds(g * 40 + l, 8, stride=5), :]
                    elif abs(m) == 1:
                        ys[m] = z1[side, pl.ds(g * 32 + l - 1, 8, stride=4), :]
                    else:
                        ys[m] = z2[side, pl.ds(g * 24 + l - 2, 8, stride=3), :]
                for n in range(2 * l + 1):
                    acc = None
                    for m in ms:
                        term = wframes[blk, SLOTS[(l, m, n)][0]] * ys[m]
                        acc = term if acc is None else acc + term
                    nat[blk, pl.ds(g * 400 + p * 25 + l * l + n, 8, stride=50), :] = acc
        return 0

    lax.fori_loop(0, groups * (edges // 128), rotate_out, 0)

    scatter = (edst_ref[...] == lax.broadcasted_iota(jnp.int32, (atoms, edges), 0)).astype(BF16)

    def aggregate(i, _):
        at = pl.multiple_of(i * step, 128)
        msgs = jnp.concatenate(
            [nat[blk, pl.ds(at, step), :].astype(BF16) for blk in range(edges // 128)], axis=1
        )
        out_ref[:, pl.ds(at, step)] = dot(scatter, msgs, 1, 1).astype(BF16)
        return 0

    lax.fori_loop(0, 2 * half // step, aggregate, 0)


def messages(core, esrc, edst, erot, ew, rot_table, mixes, own, oth):
    edges = esrc.shape[-1]
    atoms, half = own[0].shape
    row = lambda a: a.reshape(1, -1)
    vmem = pl.BlockSpec(memory_space=pltpu.VMEM)
    return pl.pallas_call(
        message_kernel,
        out_shape=jax.ShapeDtypeStruct((atoms, 2 * half), BF16),
        in_specs=[pl.BlockSpec(memory_space=pltpu.SMEM)] + [pl.BlockSpec(memory_space=pltpu.HBM)] * 18,
        out_specs=vmem,
        scratch_shapes=[
            pltpu.VMEM((2, 5 * atoms, half), BF16),
            pltpu.VMEM((edges // 128, 2 * half, 128), F32),
            pltpu.VMEM((edges // 128, len(SLOTS), 8, 128), F32),
            pltpu.VMEM((edges // 128, len(SLOTS), 8, 128), F32),
            pltpu.VMEM((rot_table.shape[0], edges), F32),
            pltpu.VMEM((4, 640, 128), F32),
            pltpu.VMEM((8, 512, 128), F32),
            pltpu.VMEM((8, 384, 128), F32),
            pltpu.VMEM((640, 512), BF16),
            pltpu.VMEM((512, 1024), BF16),
            pltpu.VMEM((384, 1024), BF16),
        ]
        + [pltpu.VMEM((1, edges), jnp.int32)] * 3
        + [pltpu.VMEM((1, edges), F32), pltpu.VMEM(rot_table.shape, F32)]
        + [pltpu.VMEM(mix.shape, BF16) for mix in mixes + mixes]
        + [pltpu.SemaphoreType.DMA((18,))],
        compiler_params=pltpu.CompilerParams(vmem_limit_bytes=54 * 1024 * 1024),
        cost_estimate=pl.CostEstimate(flops=5_000_000_000, bytes_accessed=6_000_000, transcendentals=0),
        name="messages",
    )(core, row(esrc), row(edst), row(erot), row(ew), rot_table, *mixes, *own, *oth)


def head_kernel(
    core_ref, orbitals_ref, species_ref, fo_ref, fx_ref, mine_ref, recv_ref, weight_ref, target_ref,
    load_ref, loss_ref, keep_ref, send_ref,
    feats, upd,
):
    core = core_ref[0]
    atoms, half = fo_ref.shape
    feats[core] = fo_ref[...]
    feats[1 - core] = fx_ref[...]
    for h in range(2):
        cols = slice(h * half, (h + 1) * half)
        total = mine_ref[:, cols].astype(F32) + recv_ref[:, cols].astype(F32)
        upd[:, cols] = (feats[h].astype(F32) + BRANCH * total).astype(BF16)
    blocks = dot(upd[...], weight_ref[...], 1, 0)
    width = blocks.shape[1]
    species = species_ref[...]
    lanes = jnp.zeros_like(species)
    for s in range(orbitals_ref.shape[0]):
        lanes = jnp.where(species == s, orbitals_ref[s], lanes)
    square = [lax.broadcasted_iota(jnp.int32, (atoms, atoms), d) for d in (0, 1)]
    norb = jnp.sum(jnp.where(square[0] == square[1], lanes, 0), axis=1, keepdims=True)
    cols = core * width + lax.broadcasted_iota(jnp.int32, (atoms, width), 1)
    valid = ((cols // (2 * ORB)) < norb) & (((cols // 2) % ORB) < norb)
    error = jnp.where(valid, blocks - target_ref[...], 0.0)
    divisor = norb.astype(F32)
    loss_ref[...] = jnp.sum(error * error, axis=1, keepdims=True) / divisor
    dblk = (2.0 * error / divisor).astype(BF16)
    parts = load_ref.shape[0]
    share = 2 * half // parts
    for g in range(parts):
        where = (g % 2) * (parts // 2) + g // 2
        load_ref[where, :, :width] = dblk
        load_ref[where, :, width : width + share] = upd[:, g * share : (g + 1) * share]
        load_ref[where, :, width + share :] = jnp.zeros((atoms, width - share), BF16)
    keep_ref[...] = dot(dblk, weight_ref[pl.ds(pl.multiple_of(core * half, 128), half), :], 1, 1)
    send_ref[...] = dot(dblk, weight_ref[pl.ds(pl.multiple_of((1 - core) * half, 128), half), :], 1, 1).astype(BF16)


def head(core, orbitals, species, f_own, f_oth, mine, recv, weight, target, parts):
    atoms, half = f_own.shape
    smem = pl.BlockSpec(memory_space=pltpu.SMEM)
    vmem = pl.BlockSpec(memory_space=pltpu.VMEM)
    return pl.pallas_call(
        head_kernel,
        out_shape=(
            jax.ShapeDtypeStruct((parts, atoms, 2 * target.shape[1]), BF16),
            jax.ShapeDtypeStruct((atoms, 1), F32),
            jax.ShapeDtypeStruct((atoms, half), F32),
            jax.ShapeDtypeStruct((atoms, half), BF16),
        ),
        in_specs=[smem, smem] + [vmem] * 7,
        out_specs=(vmem,) * 4,
        scratch_shapes=[
            pltpu.VMEM((2, atoms, half), BF16),
            pltpu.VMEM((atoms, 2 * half), BF16),
        ],
        compiler_params=pltpu.CompilerParams(vmem_limit_bytes=32 * 1024 * 1024),
        cost_estimate=pl.CostEstimate(flops=300_000_000, bytes_accessed=6_000_000, transcendentals=0),
        name="head",
    )(core, orbitals, species.reshape(1, -1), f_own, f_oth, mine, recv, weight, target)


def leaving_kernel(sends_ref, feats_ref, *outs):
    atoms = feats_ref.shape[0]
    places = lax.broadcasted_iota(jnp.int32, (atoms, atoms), 0)
    picks = jnp.concatenate(
        [(sends_ref[q : q + 1, :] == places).astype(F32) for q in range(len(outs))], axis=1
    ).astype(BF16)
    rows = dot(picks, feats_ref[...], 0, 0).astype(BF16)
    for q, out in enumerate(outs):
        out[...] = rows[q * atoms : (q + 1) * atoms, :]


def leaving_rows(send_rows, features):
    vmem = pl.BlockSpec(memory_space=pltpu.VMEM)
    return pl.pallas_call(
        leaving_kernel,
        out_shape=(jax.ShapeDtypeStruct(features.shape, BF16),) * len(OFFSETS),
        in_specs=[vmem, vmem],
        out_specs=(vmem,) * len(OFFSETS),
        compiler_params=pltpu.CompilerParams(vmem_limit_bytes=24 * 1024 * 1024),
        name="leaving",
    )(send_rows, features)


def partial_kernel(got_ref, out_ref):
    width = got_ref.shape[1] // 2
    full = dot(got_ref[:, width:], got_ref[:, :width], 0, 0)
    out_ref[...] = full[: out_ref.shape[0]].astype(BF16)


def partial_grad(got, share):
    vmem = pl.BlockSpec(memory_space=pltpu.VMEM)
    return pl.pallas_call(
        partial_kernel,
        out_shape=jax.ShapeDtypeStruct((share, got.shape[1] // 2), BF16),
        in_specs=[vmem],
        out_specs=vmem,
        compiler_params=pltpu.CompilerParams(vmem_limit_bytes=24 * 1024 * 1024),
        name="partial_grad",
    )(got)


def shift(x, axis, by):
    count = lax.axis_size(axis)
    return lax.ppermute(x, axis, [(i, (i + by) % count) for i in range(count)])


def plane_shift(x, early, by):
    pairs = []
    for y in range(4):
        for x_at in range(4):
            for c in range(2):
                along_x = (c == 0) == early
                to = (y, (x_at + by) % 4) if along_x else ((y + by) % 4, x_at)
                pairs.append(((y * 4 + x_at) * 2 + c, (to[0] * 4 + to[1]) * 2 + c))
    return lax.ppermute(x, ("y", "x", "chan"), pairs)


def assemble_kernel(place_ref, *refs):
    halves, out_ref, sems = refs[:8], refs[8], refs[9]
    y, x, core = place_ref[0], place_ref[1], place_ref[2]
    rows = out_ref.shape[0] // 16
    copies = []
    for late in range(4):
        for early in range(4):
            ref, at = halves[2 * late + early // 2], early % 2
            dy = late + core * (early - late)
            dx = early + core * (late - early)
            spot = lax.rem(y + 4 - dy, 4) * 4 + lax.rem(x + 4 - dx, 4)
            copies.append(
                pltpu.make_async_copy(
                    ref.at[pl.ds(at * rows, rows), :],
                    out_ref.at[pl.ds(pl.multiple_of(spot * rows, 16), rows), :],
                    sems.at[len(copies)],
                )
            )
    for copy in copies:
        copy.start()
    for copy in copies:
        copy.wait()


def assemble(place, blocks):
    rows, width = 2 * blocks[0].shape[0], blocks[0].shape[1]
    return pl.pallas_call(
        assemble_kernel,
        out_shape=jax.ShapeDtypeStruct((4 * rows, width), BF16),
        in_specs=[pl.BlockSpec(memory_space=pltpu.SMEM)]
        + [pl.BlockSpec(memory_space=pltpu.VMEM)] * len(blocks),
        out_specs=pl.BlockSpec(memory_space=pl.ANY),
        scratch_shapes=[pltpu.SemaphoreType.DMA((16,))],
        compiler_params=pltpu.CompilerParams(vmem_limit_bytes=16 * 1024 * 1024),
        name="assemble",
    )(place, *blocks)


def body(
    features, send_rows, edge_source, edge_dest, edge_rot, edge_weight, rot_table,
    mix_zero, mix_one, mix_two, atom_species, species_orbitals, head_weight, target_blocks,
):
    core = lax.axis_index("chan").astype(jnp.int32).reshape(1)
    f_oth = shift(features, "chan", 1)
    leaving = leaving_rows(send_rows, features)
    halo = [shift(leaving[OFFSETS.index(off)], ATOMS, off) for off in HALO_ORDER]
    halo_oth = [shift(h, "chan", 1) for h in halo]
    mine = messages(
        core, edge_source, edge_dest, edge_rot, edge_weight, rot_table.T,
        (mix_zero, mix_one, mix_two), [features] + halo, [f_oth] + halo_oth,
    )
    recv = shift(mine, "chan", 1)
    parts = lax.axis_size(GROUP)
    load, loss, keep, send = head(
        core, species_orbitals, atom_species, features, f_oth, mine, recv, head_weight, target_blocks, parts
    )
    got = lax.all_to_all(load, GROUP, split_axis=0, concat_axis=0, tiled=True)
    share = 2 * features.shape[1] // parts
    part = partial_grad(got.reshape(-1, got.shape[2]), share)
    part, loss, send = lax.optimization_barrier((part, loss, send))
    sums = [shift(part, "zh", by) for by in (1, -1, 2)]
    loss_oth, feat_oth = shift(loss[:, 0], "chan", 1), shift(send, "chan", 1)
    sums, loss_oth, feat_oth = lax.optimization_barrier((sums, loss_oth, feat_oth))
    near = sums[0].astype(F32) + sums[1].astype(F32)
    total = (part.astype(F32) + sums[2].astype(F32) + near).astype(BF16)
    atom_loss = loss[:, 0] + loss_oth
    grad_features = keep + feat_oth.astype(F32)
    twin = shift(total, "zl", 1)
    first = lax.axis_index("zl") == 0
    pair = jnp.concatenate([jnp.where(first, total, twin), jnp.where(first, twin, total)], axis=0)

    early = {by: plane_shift(pair, True, by) for by in (1, -1, 2)}
    low = jnp.concatenate([pair, early[1]], axis=0)
    low_behind = plane_shift(low, False, 1)
    low_ahead = plane_shift(low, False, -1)
    high = jnp.concatenate([early[2], early[-1]], axis=0)
    high_ahead = plane_shift(high, False, -1)
    high_behind = plane_shift(high, False, 1)
    low_far = plane_shift(low_behind, False, 1)
    high_far = plane_shift(high_ahead, False, -1)
    place = jnp.stack([lax.axis_index(name) for name in ("y", "x", "chan")]).astype(jnp.int32)
    grad_head = assemble(
        place, [low, high, low_behind, high_behind, low_far, high_far, low_ahead, high_ahead]
    )
    return (atom_loss, grad_head, grad_features)


def solution(mesh):
    fine = Mesh(mesh.devices.reshape(4, 2, 4, 4, 2), ("zh", "zl", "y", "x", "chan"))
    both = ATOMS + ("chan",)
    return jax.shard_map(
        body,
        mesh=fine,
        in_specs=(
            P(ATOMS, "chan"), P(ATOMS, None), P(both), P(both), P(both), P(both),
            P(), P(), P(), P(), P(ATOMS), P(), P(None, "chan"), P(ATOMS, "chan"),
        ),
        out_specs=(P(ATOMS), P(None, "chan"), P(ATOMS, "chan")),
        check_vma=False,
    )
```

```python
import functools
import jax
import jax.numpy as jnp
import numpy as np
from jax import lax
from jax.experimental import pallas as pl
from jax.experimental.pallas import tpu as pltpu
from jax.sharding import Mesh, PartitionSpec as P

ORB = 16
LMAX = 4
MMAX = 2
OFFSETS = (1, -1, 2, -2)
HALO_ORDER = (1, 2, -1, -2)
BRANCH = 0.125
PREP_MB = 56
MSG_MB = 54
GROUP = ("zl", "y", "x")
ATOMS = ("zh", "zl", "y", "x")
F32 = jnp.float32
BF16 = jnp.bfloat16


def frame_entries():
    slots = {}
    start = 0
    for l in range(LMAX + 1):
        width = 2 * l + 1
        for m in range(-min(l, MMAX), min(l, MMAX) + 1):
            for n in range(width):
                slots[(l, m, n)] = (len(slots), start + (l + m) * width + n)
        start += width * width
    return slots


SLOTS = frame_entries()


def dot(a, b, ca, cb):
    return lax.dot_general(a, b, (((ca,), (cb,)), ((), ())), preferred_element_type=F32)


def prepare_kernel(
    esrc_hbm, edst_hbm, erot_hbm, ew_hbm, rot_hbm, mix0_hbm, mix1_hbm, mix2_hbm,
    frames, wframes, onehot_ref, scatter_ref, mix0_ref, mix1_ref, mix2_ref,
    packed, esrc_ref, edst_ref, erot_ref, ew_ref, rot_ref, mix0_in, mix1_in, mix2_in, sems,
):
    copies = [
        pltpu.make_async_copy(src, dst, sems.at[i])
        for i, (src, dst) in enumerate(
            (
                (erot_hbm, erot_ref), (ew_hbm, ew_ref), (rot_hbm, rot_ref), (esrc_hbm, esrc_ref),
                (edst_hbm, edst_ref), (mix0_hbm, mix0_in), (mix1_hbm, mix1_in), (mix2_hbm, mix2_in),
            )
        )
    ]
    for copy in copies:
        copy.start()
    for copy in copies[:5]:
        copy.wait()
    edges = esrc_ref.shape[1]

    onehot_ref[...] = (esrc_ref[...] == lax.broadcasted_iota(jnp.int32, onehot_ref.shape, 0)).astype(BF16)
    scatter_ref[...] = (edst_ref[...] == lax.broadcasted_iota(jnp.int32, scatter_ref.shape, 0)).astype(BF16)

    rot_count = rot_ref.shape[1]
    picks = (erot_ref[...] == lax.broadcasted_iota(jnp.int32, (rot_count, edges), 0)).astype(BF16)
    rot = rot_ref[...]
    rot_hi = rot.astype(BF16)
    rot_lo = (rot - rot_hi.astype(F32)).astype(BF16)
    packed[...] = dot(rot_hi, picks, 1, 0) + dot(rot_lo, picks, 1, 0)
    for blk in range(edges // 128):
        lanes = slice(blk * 128, (blk + 1) * 128)
        weight = jnp.broadcast_to(ew_ref[:, lanes], (8, 128))
        for slot, entry in SLOTS.values():
            value = jnp.broadcast_to(packed[entry : entry + 1, lanes], (8, 128))
            frames[blk, slot] = value
            wframes[blk, slot] = value * weight

    for copy in copies[5:]:
        copy.wait()
    mix0_ref[...] = mix0_in[...].T
    for i in range(2):
        mix1_ref[i] = mix1_in[i].T
        mix2_ref[i] = mix2_in[i].T


def prepare(esrc, edst, erot, ew, rot_table, mixes, atoms):
    edges = esrc.shape[-1]
    row = lambda a: a.reshape(1, -1)
    vmem = pl.BlockSpec(memory_space=pltpu.VMEM)
    frames = jax.ShapeDtypeStruct((edges // 128, len(SLOTS), 8, 128), F32)
    return pl.pallas_call(
        prepare_kernel,
        out_shape=(
            frames, frames,
            jax.ShapeDtypeStruct((5 * atoms, edges), BF16),
            jax.ShapeDtypeStruct((atoms, edges), BF16),
        )
        + tuple(jax.ShapeDtypeStruct(mix.shape, BF16) for mix in mixes),
        in_specs=[pl.BlockSpec(memory_space=pl.ANY)] * 8,
        out_specs=(vmem,) * 7,
        scratch_shapes=[pltpu.VMEM((rot_table.shape[0], edges), F32)]
        + [pltpu.VMEM((1, edges), jnp.int32)] * 3
        + [pltpu.VMEM((1, edges), F32), pltpu.VMEM(rot_table.shape, F32)]
        + [pltpu.VMEM(mix.shape, BF16) for mix in mixes]
        + [pltpu.SemaphoreType.DMA((8,))],
        compiler_params=pltpu.CompilerParams(vmem_limit_bytes=PREP_MB * 1024 * 1024),
        cost_estimate=pl.CostEstimate(flops=100_000_000, bytes_accessed=10_000_000, transcendentals=0),
        name="prepare",
    )(row(esrc), row(edst), row(erot), row(ew), rot_table, *mixes)


def message_kernel(
    core_ref, frames_hbm, wframes_hbm, onehot_hbm, scatter_hbm, mix0_hbm, mix1_hbm, mix2_hbm,
    fo_ref, ho0_ref, ho1_ref, ho2_ref, ho3_ref,
    fx_ref, hx0_ref, hx1_ref, hx2_ref, hx3_ref,
    out_ref,
    rows, nat, z0, z1, z2, xb0, xb1, xb2,
    frames, wframes, onehot_ref, scatter_ref, mix0_ref, mix1_ref, mix2_ref, sems,
):
    core = core_ref[0]
    other = 1 - core
    pick, frame, wframe, place, *mixes = [
        pltpu.make_async_copy(src, dst, sems.at[10 + i])
        for i, (src, dst) in enumerate(
            (
                (onehot_hbm, onehot_ref), (frames_hbm, frames), (wframes_hbm, wframes),
                (scatter_hbm, scatter_ref), (mix0_hbm, mix0_ref), (mix1_hbm, mix1_ref), (mix2_hbm, mix2_ref),
            )
        )
    ]
    edges = onehot_ref.shape[1]
    atoms, half = fo_ref.shape

    moves = []
    for q, (own, oth) in enumerate(
        zip((fo_ref, ho0_ref, ho1_ref, ho2_ref, ho3_ref), (fx_ref, hx0_ref, hx1_ref, hx2_ref, hx3_ref))
    ):
        at = pl.ds(0 if q == 0 else (1 + OFFSETS.index(HALO_ORDER[q - 1])) * atoms, atoms)
        moves.append(pltpu.make_async_copy(own, rows.at[core, at, :], sems.at[2 * q]))
        moves.append(pltpu.make_async_copy(oth, rows.at[other, at, :], sems.at[2 * q + 1]))
    for move in [pick] + moves + [frame] + mixes + [wframe, place]:
        move.start()
    pick.wait()
    onehot = onehot_ref[...]

    step = 640

    def gather(i, _):
        h = i // (half // step)
        n = i % (half // step)
        got = dot(rows[h, :, pl.ds(pl.multiple_of(n * step, 128), step)], onehot, 0, 0)
        at = pl.multiple_of(i * step, 8)
        for blk in range(edges // 128):
            nat[blk, pl.ds(at, step), :] = got[:, blk * 128 : (blk + 1) * 128]
        return 0

    for move in moves:
        move.wait()
    lax.fori_loop(0, 2 * half // step, gather, 0)

    groups = 2 * half // 400

    def rotate_in(i, _):
        blk = i // groups
        g = i % groups
        for p in range(2):
            nb = blk * 2 + p
            for l in range(LMAX + 1):
                xs = [nat[blk, pl.ds(g * 400 + p * 25 + l * l + n, 8, stride=50), :] for n in range(2 * l + 1)]
                for m in range(-min(l, MMAX), min(l, MMAX) + 1):
                    acc = frames[blk, SLOTS[(l, m, 0)][0]] * xs[0]
                    for n in range(1, 2 * l + 1):
                        acc = acc + frames[blk, SLOTS[(l, m, n)][0]] * xs[n]
                    if m == 0:
                        z0[nb, pl.ds(g * 40 + l, 8, stride=5), :] = acc
                    else:
                        side = nb if m > 0 else nb + 4
                        if abs(m) == 1:
                            z1[side, pl.ds(g * 32 + l - 1, 8, stride=4), :] = acc
                        else:
                            z2[side, pl.ds(g * 24 + l - 2, 8, stride=3), :] = acc
        return 0

    frame.wait()
    lax.fori_loop(0, groups * (edges // 128), rotate_in, 0)

    for nb in range(4):
        xb0[:, nb * 128 : (nb + 1) * 128] = z0[nb].astype(BF16)
    for nb in range(8):
        xb1[:, nb * 128 : (nb + 1) * 128] = z1[nb].astype(BF16)
        xb2[:, nb * 128 : (nb + 1) * 128] = z2[nb].astype(BF16)

    def mix_zero(n, _):
        y = dot(mix0_ref[...], xb0[:, pl.ds(pl.multiple_of(n * 256, 256), 256)], 1, 0)
        z0[2 * n] = y[:, :128]
        z0[2 * n + 1] = y[:, 128:]
        return 0

    for mix in mixes:
        mix.wait()
    lax.fori_loop(0, 2, mix_zero, 0)

    def mix_pair(mix_ref, xb, z):
        def part(n, _):
            plus = xb[:, pl.ds(pl.multiple_of(n * 256, 256), 256)]
            minus = xb[:, pl.ds(pl.multiple_of(n * 256 + 512, 256), 256)]
            y = dot(mix_ref[0], plus, 1, 0) - dot(mix_ref[1], minus, 1, 0)
            z[2 * n] = y[:, :128]
            z[2 * n + 1] = y[:, 128:]
            y = dot(mix_ref[0], minus, 1, 0) + dot(mix_ref[1], plus, 1, 0)
            z[2 * n + 4] = y[:, :128]
            z[2 * n + 5] = y[:, 128:]
            return 0

        lax.fori_loop(0, 2, part, 0)

    mix_pair(mix1_ref, xb1, z1)
    mix_pair(mix2_ref, xb2, z2)

    def rotate_out(i, _):
        blk = i // groups
        g = i % groups
        for p in range(2):
            nb = blk * 2 + p
            for l in range(LMAX + 1):
                ms = range(-min(l, MMAX), min(l, MMAX) + 1)
                ys = {}
                for m in ms:
                    side = nb if m >= 0 else nb + 4
                    if m == 0:
                        ys[m] = z0[nb, pl.ds(g * 40 + l, 8, stride=5), :]
                    elif abs(m) == 1:
                        ys[m] = z1[side, pl.ds(g * 32 + l - 1, 8, stride=4), :]
                    else:
                        ys[m] = z2[side, pl.ds(g * 24 + l - 2, 8, stride=3), :]
                for n in range(2 * l + 1):
                    acc = None
                    for m in ms:
                        term = wframes[blk, SLOTS[(l, m, n)][0]] * ys[m]
                        acc = term if acc is None else acc + term
                    nat[blk, pl.ds(g * 400 + p * 25 + l * l + n, 8, stride=50), :] = acc
        return 0

    wframe.wait()
    lax.fori_loop(0, groups * (edges // 128), rotate_out, 0)
    place.wait()

    scatter = scatter_ref[...]

    def aggregate(i, _):
        at = pl.multiple_of(i * step, 128)
        msgs = jnp.concatenate(
            [nat[blk, pl.ds(at, step), :].astype(BF16) for blk in range(edges // 128)], axis=1
        )
        out_ref[:, pl.ds(at, step)] = dot(scatter, msgs, 1, 1).astype(BF16)
        return 0

    lax.fori_loop(0, 2 * half // step, aggregate, 0)


def messages(core, prepared, own, oth):
    edges = prepared[2].shape[1]
    atoms, half = own[0].shape
    vmem = pl.BlockSpec(memory_space=pltpu.VMEM)
    return pl.pallas_call(
        message_kernel,
        out_shape=jax.ShapeDtypeStruct((atoms, 2 * half), BF16),
        in_specs=[pl.BlockSpec(memory_space=pltpu.SMEM)]
        + [pl.BlockSpec(memory_space=pl.ANY)] * (len(prepared) + 10),
        out_specs=vmem,
        scratch_shapes=[
            pltpu.VMEM((2, 5 * atoms, half), BF16),
            pltpu.VMEM((edges // 128, 2 * half, 128), F32),
            pltpu.VMEM((4, 640, 128), F32),
            pltpu.VMEM((8, 512, 128), F32),
            pltpu.VMEM((8, 384, 128), F32),
            pltpu.VMEM((640, 512), BF16),
            pltpu.VMEM((512, 1024), BF16),
            pltpu.VMEM((384, 1024), BF16),
        ]
        + [pltpu.VMEM(table.shape, table.dtype) for table in prepared]
        + [pltpu.SemaphoreType.DMA((17,))],
        compiler_params=pltpu.CompilerParams(vmem_limit_bytes=MSG_MB * 1024 * 1024),
        cost_estimate=pl.CostEstimate(flops=5_000_000_000, bytes_accessed=6_000_000, transcendentals=0),
        name="messages",
    )(core, *prepared, *own, *oth)


def head_kernel(
    core_ref, orbitals_ref, species_ref, fo_ref, fx_ref, mine_ref, recv_ref, weight_ref, target_ref,
    load_ref, loss_ref, keep_ref, send_ref,
    feats, upd,
):
    core = core_ref[0]
    atoms, half = fo_ref.shape
    feats[core] = fo_ref[...]
    feats[1 - core] = fx_ref[...]
    for h in range(2):
        cols = slice(h * half, (h + 1) * half)
        total = mine_ref[:, cols].astype(F32) + recv_ref[:, cols].astype(F32)
        upd[:, cols] = (feats[h].astype(F32) + BRANCH * total).astype(BF16)
    blocks = dot(upd[...], weight_ref[...], 1, 0)
    width = blocks.shape[1]
    species = species_ref[...]
    lanes = jnp.zeros_like(species)
    for s in range(orbitals_ref.shape[0]):
        lanes = jnp.where(species == s, orbitals_ref[s], lanes)
    square = [lax.broadcasted_iota(jnp.int32, (atoms, atoms), d) for d in (0, 1)]
    norb = jnp.sum(jnp.where(square[0] == square[1], lanes, 0), axis=1, keepdims=True)
    cols = core * width + lax.broadcasted_iota(jnp.int32, (atoms, width), 1)
    valid = ((cols // (2 * ORB)) < norb) & (((cols // 2) % ORB) < norb)
    error = jnp.where(valid, blocks - target_ref[...], 0.0)
    divisor = norb.astype(F32)
    loss_ref[...] = jnp.sum(error * error, axis=1, keepdims=True) / divisor
    dblk = (2.0 * error / divisor).astype(BF16)
    parts = load_ref.shape[0]
    share = 2 * half // parts
    for g in range(parts):
        where = (g % 2) * (parts // 2) + g // 2
        load_ref[where, :, :width] = dblk
        load_ref[where, :, width : width + share] = upd[:, g * share : (g + 1) * share]
        load_ref[where, :, width + share :] = jnp.zeros((atoms, width - share), BF16)
    keep_ref[...] = dot(dblk, weight_ref[pl.ds(pl.multiple_of(core * half, 128), half), :], 1, 1)
    send_ref[...] = dot(dblk, weight_ref[pl.ds(pl.multiple_of((1 - core) * half, 128), half), :], 1, 1).astype(BF16)


def head(core, orbitals, species, f_own, f_oth, mine, recv, weight, target, parts):
    atoms, half = f_own.shape
    smem = pl.BlockSpec(memory_space=pltpu.SMEM)
    vmem = pl.BlockSpec(memory_space=pltpu.VMEM)
    return pl.pallas_call(
        head_kernel,
        out_shape=(
            jax.ShapeDtypeStruct((parts, atoms, 2 * target.shape[1]), BF16),
            jax.ShapeDtypeStruct((atoms, 1), F32),
            jax.ShapeDtypeStruct((atoms, half), F32),
            jax.ShapeDtypeStruct((atoms, half), BF16),
        ),
        in_specs=[smem, smem] + [vmem] * 7,
        out_specs=(vmem,) * 4,
        scratch_shapes=[
            pltpu.VMEM((2, atoms, half), BF16),
            pltpu.VMEM((atoms, 2 * half), BF16),
        ],
        compiler_params=pltpu.CompilerParams(vmem_limit_bytes=32 * 1024 * 1024),
        cost_estimate=pl.CostEstimate(flops=300_000_000, bytes_accessed=6_000_000, transcendentals=0),
        name="head",
    )(core, orbitals, species.reshape(1, -1), f_own, f_oth, mine, recv, weight, target)


def leaving_kernel(sends_ref, feats_ref, *outs):
    atoms = feats_ref.shape[0]
    places = lax.broadcasted_iota(jnp.int32, (atoms, atoms), 0)
    picks = jnp.concatenate(
        [(sends_ref[q : q + 1, :] == places).astype(F32) for q in range(len(outs))], axis=1
    ).astype(BF16)
    rows = dot(picks, feats_ref[...], 0, 0).astype(BF16)
    for q, out in enumerate(outs):
        out[...] = rows[q * atoms : (q + 1) * atoms, :]


def leaving_rows(send_rows, features):
    vmem = pl.BlockSpec(memory_space=pltpu.VMEM)
    return pl.pallas_call(
        leaving_kernel,
        out_shape=(jax.ShapeDtypeStruct(features.shape, BF16),) * len(OFFSETS),
        in_specs=[vmem, vmem],
        out_specs=(vmem,) * len(OFFSETS),
        compiler_params=pltpu.CompilerParams(vmem_limit_bytes=24 * 1024 * 1024),
        name="leaving",
    )(send_rows, features)


def partial_kernel(got_ref, out_ref):
    width = got_ref.shape[1] // 2
    full = dot(got_ref[:, width:], got_ref[:, :width], 0, 0)
    out_ref[...] = full[: out_ref.shape[0]].astype(BF16)


def partial_grad(got, share):
    vmem = pl.BlockSpec(memory_space=pltpu.VMEM)
    return pl.pallas_call(
        partial_kernel,
        out_shape=jax.ShapeDtypeStruct((share, got.shape[1] // 2), BF16),
        in_specs=[vmem],
        out_specs=vmem,
        compiler_params=pltpu.CompilerParams(vmem_limit_bytes=24 * 1024 * 1024),
        name="partial_grad",
    )(got)


def shift(x, axis, by):
    count = lax.axis_size(axis)
    return lax.ppermute(x, axis, [(i, (i + by) % count) for i in range(count)])


def plane_shift(x, early, by):
    pairs = []
    for y in range(4):
        for x_at in range(4):
            for c in range(2):
                along_x = (c == 0) == early
                to = (y, (x_at + by) % 4) if along_x else ((y + by) % 4, x_at)
                pairs.append(((y * 4 + x_at) * 2 + c, (to[0] * 4 + to[1]) * 2 + c))
    return lax.ppermute(x, ("y", "x", "chan"), pairs)


def assemble_kernel(lates, place_ref, *refs):
    halves, out_ref, sems = refs[: 2 * len(lates)], refs[-2], refs[-1]
    y, x, core = place_ref[0], place_ref[1], place_ref[2]
    rows = out_ref.shape[0] // 16
    copies = []
    for i, late in enumerate(lates):
        for early in range(4):
            dy = late + core * (early - late)
            dx = early + core * (late - early)
            spot = lax.rem(y + 4 - dy, 4) * 4 + lax.rem(x + 4 - dx, 4)
            copies.append(
                pltpu.make_async_copy(
                    halves[2 * i + early // 2].at[pl.ds(early % 2 * rows, rows), :],
                    out_ref.at[pl.ds(pl.multiple_of(spot * rows, 16), rows), :],
                    sems.at[len(copies)],
                )
            )
    for copy in copies:
        copy.start()
    for copy in copies:
        copy.wait()


def assemble(place, lates, halves, into=None):
    rows, width = halves[0].shape
    hbm = pl.BlockSpec(memory_space=pl.ANY)
    given = [] if into is None else [into]
    return pl.pallas_call(
        functools.partial(assemble_kernel, lates),
        out_shape=jax.ShapeDtypeStruct((8 * rows, width), BF16),
        in_specs=[pl.BlockSpec(memory_space=pltpu.SMEM)]
        + [pl.BlockSpec(memory_space=pltpu.VMEM)] * len(halves)
        + [hbm] * len(given),
        out_specs=hbm,
        input_output_aliases={1 + len(halves): 0} if given else {},
        scratch_shapes=[pltpu.SemaphoreType.DMA((4 * len(lates),))],
        compiler_params=pltpu.CompilerParams(vmem_limit_bytes=16 * 1024 * 1024),
        name="assemble",
    )(place, *halves, *given)


def body(
    features, send_rows, edge_source, edge_dest, edge_rot, edge_weight, rot_table,
    mix_zero, mix_one, mix_two, atom_species, species_orbitals, head_weight, target_blocks,
):
    core = lax.axis_index("chan").astype(jnp.int32).reshape(1)
    leaving = leaving_rows(send_rows, features)
    halo = [shift(leaving[OFFSETS.index(off)], ATOMS, off) for off in HALO_ORDER]
    prepared = prepare(
        edge_source, edge_dest, edge_rot, edge_weight, rot_table.T,
        (mix_zero, mix_one, mix_two), features.shape[0],
    )
    features, prepared = lax.optimization_barrier((features, prepared))
    f_oth = shift(features, "chan", 1)
    halo_oth = [shift(h, "chan", 1) for h in halo]
    mine = messages(core, prepared, [features] + halo, [f_oth] + halo_oth)
    recv = shift(mine, "chan", 1)
    parts = lax.axis_size(GROUP)
    load, loss, keep, send = head(
        core, species_orbitals, atom_species, features, f_oth, mine, recv, head_weight, target_blocks, parts
    )
    got = lax.all_to_all(load, GROUP, split_axis=0, concat_axis=0, tiled=True)
    share = 2 * features.shape[1] // parts
    part = partial_grad(got.reshape(-1, got.shape[2]), share)
    part, loss, send = lax.optimization_barrier((part, loss, send))
    sums = [shift(part, "zh", by) for by in (1, -1, 2)]
    loss_oth, feat_oth = shift(loss[:, 0], "chan", 1), shift(send, "chan", 1)
    sums, loss_oth, feat_oth = lax.optimization_barrier((sums, loss_oth, feat_oth))
    near = sums[0].astype(F32) + sums[1].astype(F32)
    total = (part.astype(F32) + sums[2].astype(F32) + near).astype(BF16)
    atom_loss = loss[:, 0] + loss_oth
    grad_features = keep + feat_oth.astype(F32)
    twin = shift(total, "zl", 1)
    first = lax.axis_index("zl") == 0
    pair = jnp.concatenate([jnp.where(first, total, twin), jnp.where(first, twin, total)], axis=0)

    early = {by: plane_shift(pair, True, by) for by in (1, -1, 2)}
    low = jnp.concatenate([pair, early[1]], axis=0)
    low_behind = plane_shift(low, False, 1)
    low_ahead = plane_shift(low, False, -1)
    high = jnp.concatenate([early[2], early[-1]], axis=0)
    high_ahead = plane_shift(high, False, -1)
    high_behind = plane_shift(high, False, 1)
    low_far = plane_shift(low_behind, False, 1)
    high_far = plane_shift(high_ahead, False, -1)
    place = jnp.stack([lax.axis_index(name) for name in ("y", "x", "chan")]).astype(jnp.int32)
    grad_head = assemble(
        place, (0, 1, 3), [low, high, low_behind, high_behind, low_ahead, high_ahead]
    )
    grad_head = assemble(place, (2,), [low_far, high_far], grad_head)
    return (atom_loss, grad_head, grad_features)


def solution(mesh):
    fine = Mesh(mesh.devices.reshape(4, 2, 4, 4, 2), ("zh", "zl", "y", "x", "chan"))
    both = ATOMS + ("chan",)
    return jax.shard_map(
        body,
        mesh=fine,
        in_specs=(
            P(ATOMS, "chan"), P(ATOMS, None), P(both), P(both), P(both), P(both),
            P(), P(), P(), P(), P(ATOMS), P(), P(None, "chan"), P(ATOMS, "chan"),
        ),
        out_specs=(P(ATOMS), P(None, "chan"), P(ATOMS, "chan")),
        check_vma=False,
    )
```

```python
import functools
import jax
import jax.numpy as jnp
import numpy as np
from jax import lax
from jax.experimental import pallas as pl
from jax.experimental.pallas import tpu as pltpu
from jax.sharding import Mesh, PartitionSpec as P

ORB = 16
LMAX = 4
MMAX = 2
OFFSETS = (1, -1, 2, -2)
HALO_ORDER = (1, 2, -1, -2)
BRANCH = 0.125
PREP_MB = 56
MSG_MB = 54
GROUP = ("zl", "y", "x")
ATOMS = ("zh", "zl", "y", "x")
F32 = jnp.float32
BF16 = jnp.bfloat16


def frame_entries():
    slots = {}
    start = 0
    for l in range(LMAX + 1):
        width = 2 * l + 1
        for m in range(-min(l, MMAX), min(l, MMAX) + 1):
            for n in range(width):
                slots[(l, m, n)] = (len(slots), start + (l + m) * width + n)
        start += width * width
    return slots


SLOTS = frame_entries()


def dot(a, b, ca, cb):
    return lax.dot_general(a, b, (((ca,), (cb,)), ((), ())), preferred_element_type=F32)


def prepare_kernel(
    esrc_hbm, edst_hbm, erot_hbm, ew_hbm, rot_hbm, mix0_hbm, mix1_hbm, mix2_hbm,
    frames, wframes, onehot_ref, scatter_ref, mix0_ref, mix1_ref, mix2_ref,
    packed, esrc_ref, edst_ref, erot_ref, ew_ref, rot_ref, mix0_in, mix1_in, mix2_in, sems,
):
    copies = [
        pltpu.make_async_copy(src, dst, sems.at[i])
        for i, (src, dst) in enumerate(
            (
                (erot_hbm, erot_ref), (ew_hbm, ew_ref), (rot_hbm, rot_ref), (esrc_hbm, esrc_ref),
                (edst_hbm, edst_ref), (mix0_hbm, mix0_in), (mix1_hbm, mix1_in), (mix2_hbm, mix2_in),
            )
        )
    ]
    for copy in copies:
        copy.start()
    for copy in copies[:5]:
        copy.wait()
    edges = esrc_ref.shape[1]

    onehot_ref[...] = (esrc_ref[...] == lax.broadcasted_iota(jnp.int32, onehot_ref.shape, 0)).astype(BF16)
    scatter_ref[...] = (edst_ref[...] == lax.broadcasted_iota(jnp.int32, scatter_ref.shape, 0)).astype(BF16)

    rot_count = rot_ref.shape[1]
    picks = (erot_ref[...] == lax.broadcasted_iota(jnp.int32, (rot_count, edges), 0)).astype(BF16)
    rot = rot_ref[...]
    rot_hi = rot.astype(BF16)
    rot_lo = (rot - rot_hi.astype(F32)).astype(BF16)
    packed[...] = dot(rot_hi, picks, 1, 0) + dot(rot_lo, picks, 1, 0)
    for blk in range(edges // 128):
        lanes = slice(blk * 128, (blk + 1) * 128)
        weight = jnp.broadcast_to(ew_ref[:, lanes], (8, 128))
        for slot, entry in SLOTS.values():
            value = jnp.broadcast_to(packed[entry : entry + 1, lanes], (8, 128))
            frames[blk, slot] = value
            wframes[blk, slot] = value * weight

    for copy in copies[5:]:
        copy.wait()
    mix0_ref[...] = mix0_in[...].T
    for i in range(2):
        mix1_ref[i] = mix1_in[i].T
        mix2_ref[i] = mix2_in[i].T


def prepare(esrc, edst, erot, ew, rot_table, mixes, atoms):
    edges = esrc.shape[-1]
    row = lambda a: a.reshape(1, -1)
    vmem = pl.BlockSpec(memory_space=pltpu.VMEM)
    frames = jax.ShapeDtypeStruct((edges // 128, len(SLOTS), 8, 128), F32)
    return pl.pallas_call(
        prepare_kernel,
        out_shape=(
            frames, frames,
            jax.ShapeDtypeStruct((5 * atoms, edges), BF16),
            jax.ShapeDtypeStruct((atoms, edges), BF16),
        )
        + tuple(jax.ShapeDtypeStruct(mix.shape, BF16) for mix in mixes),
        in_specs=[pl.BlockSpec(memory_space=pl.ANY)] * 8,
        out_specs=(vmem,) * 7,
        scratch_shapes=[pltpu.VMEM((rot_table.shape[0], edges), F32)]
        + [pltpu.VMEM((1, edges), jnp.int32)] * 3
        + [pltpu.VMEM((1, edges), F32), pltpu.VMEM(rot_table.shape, F32)]
        + [pltpu.VMEM(mix.shape, BF16) for mix in mixes]
        + [pltpu.SemaphoreType.DMA((8,))],
        compiler_params=pltpu.CompilerParams(vmem_limit_bytes=PREP_MB * 1024 * 1024),
        cost_estimate=pl.CostEstimate(flops=100_000_000, bytes_accessed=10_000_000, transcendentals=0),
        name="prepare",
    )(row(esrc), row(edst), row(erot), row(ew), rot_table, *mixes)


def message_kernel(
    core_ref, frames_hbm, wframes_hbm, onehot_hbm, scatter_hbm, mix0_hbm, mix1_hbm, mix2_hbm,
    fo_ref, ho0_ref, ho1_ref, ho2_ref, ho3_ref,
    fx_ref, hx0_ref, hx1_ref, hx2_ref, hx3_ref,
    out_ref,
    rows, nat, z0, z1, z2, xb0, xb1, xb2,
    frames, wframes, onehot_ref, scatter_ref, mix0_ref, mix1_ref, mix2_ref, sems,
):
    core = core_ref[0]
    other = 1 - core
    pick, frame, wframe, place, *mixes = [
        pltpu.make_async_copy(src, dst, sems.at[10 + i])
        for i, (src, dst) in enumerate(
            (
                (onehot_hbm, onehot_ref), (frames_hbm, frames), (wframes_hbm, wframes),
                (scatter_hbm, scatter_ref), (mix0_hbm, mix0_ref), (mix1_hbm, mix1_ref), (mix2_hbm, mix2_ref),
            )
        )
    ]
    edges = onehot_ref.shape[1]
    atoms, half = fo_ref.shape

    moves = []
    for q, (own, oth) in enumerate(
        zip((fo_ref, ho0_ref, ho1_ref, ho2_ref, ho3_ref), (fx_ref, hx0_ref, hx1_ref, hx2_ref, hx3_ref))
    ):
        at = pl.ds(0 if q == 0 else (1 + OFFSETS.index(HALO_ORDER[q - 1])) * atoms, atoms)
        moves.append(pltpu.make_async_copy(own, rows.at[core, at, :], sems.at[2 * q]))
        moves.append(pltpu.make_async_copy(oth, rows.at[other, at, :], sems.at[2 * q + 1]))
    for move in [pick] + moves + [frame] + mixes + [wframe, place]:
        move.start()
    pick.wait()
    onehot = onehot_ref[...]

    step = 640

    def gather(i, _):
        h = i // (half // step)
        n = i % (half // step)
        got = dot(rows[h, :, pl.ds(pl.multiple_of(n * step, 128), step)], onehot, 0, 0)
        at = pl.multiple_of(i * step, 8)
        for blk in range(edges // 128):
            nat[blk, pl.ds(at, step), :] = got[:, blk * 128 : (blk + 1) * 128]
        return 0

    for move in moves:
        move.wait()
    lax.fori_loop(0, 2 * half // step, gather, 0, unroll=10)

    groups = 2 * half // 400

    def rotate_in(i, _):
        blk = i // groups
        g = i % groups
        for p in range(2):
            nb = blk * 2 + p
            for l in range(LMAX + 1):
                xs = [nat[blk, pl.ds(g * 400 + p * 25 + l * l + n, 8, stride=50), :] for n in range(2 * l + 1)]
                for m in range(-min(l, MMAX), min(l, MMAX) + 1):
                    acc = frames[blk, SLOTS[(l, m, 0)][0]] * xs[0]
                    for n in range(1, 2 * l + 1):
                        acc = acc + frames[blk, SLOTS[(l, m, n)][0]] * xs[n]
                    if m == 0:
                        z0[nb, pl.ds(g * 40 + l, 8, stride=5), :] = acc
                    else:
                        side = nb if m > 0 else nb + 4
                        if abs(m) == 1:
                            z1[side, pl.ds(g * 32 + l - 1, 8, stride=4), :] = acc
                        else:
                            z2[side, pl.ds(g * 24 + l - 2, 8, stride=3), :] = acc
        return 0

    frame.wait()
    lax.fori_loop(0, groups * (edges // 128), rotate_in, 0, unroll=4)

    for nb in range(4):
        xb0[:, nb * 128 : (nb + 1) * 128] = z0[nb].astype(BF16)
    for nb in range(8):
        xb1[:, nb * 128 : (nb + 1) * 128] = z1[nb].astype(BF16)
        xb2[:, nb * 128 : (nb + 1) * 128] = z2[nb].astype(BF16)

    def mix_zero(n, _):
        y = dot(mix0_ref[...], xb0[:, pl.ds(pl.multiple_of(n * 256, 256), 256)], 1, 0)
        z0[2 * n] = y[:, :128]
        z0[2 * n + 1] = y[:, 128:]
        return 0

    for mix in mixes:
        mix.wait()
    lax.fori_loop(0, 2, mix_zero, 0, unroll=True)

    def mix_pair(mix_ref, xb, z):
        def part(n, _):
            plus = xb[:, pl.ds(pl.multiple_of(n * 256, 256), 256)]
            minus = xb[:, pl.ds(pl.multiple_of(n * 256 + 512, 256), 256)]
            y = dot(mix_ref[0], plus, 1, 0) - dot(mix_ref[1], minus, 1, 0)
            z[2 * n] = y[:, :128]
            z[2 * n + 1] = y[:, 128:]
            y = dot(mix_ref[0], minus, 1, 0) + dot(mix_ref[1], plus, 1, 0)
            z[2 * n + 4] = y[:, :128]
            z[2 * n + 5] = y[:, 128:]
            return 0

        lax.fori_loop(0, 2, part, 0, unroll=True)

    mix_pair(mix1_ref, xb1, z1)
    mix_pair(mix2_ref, xb2, z2)

    def rotate_out(i, _):
        blk = i // groups
        g = i % groups
        for p in range(2):
            nb = blk * 2 + p
            for l in range(LMAX + 1):
                ms = range(-min(l, MMAX), min(l, MMAX) + 1)
                ys = {}
                for m in ms:
                    side = nb if m >= 0 else nb + 4
                    if m == 0:
                        ys[m] = z0[nb, pl.ds(g * 40 + l, 8, stride=5), :]
                    elif abs(m) == 1:
                        ys[m] = z1[side, pl.ds(g * 32 + l - 1, 8, stride=4), :]
                    else:
                        ys[m] = z2[side, pl.ds(g * 24 + l - 2, 8, stride=3), :]
                for n in range(2 * l + 1):
                    acc = None
                    for m in ms:
                        term = wframes[blk, SLOTS[(l, m, n)][0]] * ys[m]
                        acc = term if acc is None else acc + term
                    nat[blk, pl.ds(g * 400 + p * 25 + l * l + n, 8, stride=50), :] = acc
        return 0

    wframe.wait()
    lax.fori_loop(0, groups * (edges // 128), rotate_out, 0)
    place.wait()

    scatter = scatter_ref[...]

    def aggregate(i, _):
        at = pl.multiple_of(i * step, 128)
        msgs = jnp.concatenate(
            [nat[blk, pl.ds(at, step), :].astype(BF16) for blk in range(edges // 128)], axis=1
        )
        out_ref[:, pl.ds(at, step)] = dot(scatter, msgs, 1, 1).astype(BF16)
        return 0

    lax.fori_loop(0, 2 * half // step, aggregate, 0, unroll=5)


def messages(core, prepared, own, oth):
    edges = prepared[2].shape[1]
    atoms, half = own[0].shape
    vmem = pl.BlockSpec(memory_space=pltpu.VMEM)
    return pl.pallas_call(
        message_kernel,
        out_shape=jax.ShapeDtypeStruct((atoms, 2 * half), BF16),
        in_specs=[pl.BlockSpec(memory_space=pltpu.SMEM)]
        + [pl.BlockSpec(memory_space=pl.ANY)] * (len(prepared) + 10),
        out_specs=vmem,
        scratch_shapes=[
            pltpu.VMEM((2, 5 * atoms, half), BF16),
            pltpu.VMEM((edges // 128, 2 * half, 128), F32),
            pltpu.VMEM((4, 640, 128), F32),
            pltpu.VMEM((8, 512, 128), F32),
            pltpu.VMEM((8, 384, 128), F32),
            pltpu.VMEM((640, 512), BF16),
            pltpu.VMEM((512, 1024), BF16),
            pltpu.VMEM((384, 1024), BF16),
        ]
        + [pltpu.VMEM(table.shape, table.dtype) for table in prepared]
        + [pltpu.SemaphoreType.DMA((17,))],
        compiler_params=pltpu.CompilerParams(vmem_limit_bytes=MSG_MB * 1024 * 1024),
        cost_estimate=pl.CostEstimate(flops=5_000_000_000, bytes_accessed=6_000_000, transcendentals=0),
        name="messages",
    )(core, *prepared, *own, *oth)


def head_kernel(
    core_ref, orbitals_ref, species_ref, fo_ref, fx_ref, mine_ref, recv_ref, weight_ref, target_ref,
    load_ref, loss_ref, keep_ref, send_ref,
    feats, upd,
):
    core = core_ref[0]
    atoms, half = fo_ref.shape
    feats[core] = fo_ref[...]
    feats[1 - core] = fx_ref[...]
    for h in range(2):
        cols = slice(h * half, (h + 1) * half)
        total = mine_ref[:, cols].astype(F32) + recv_ref[:, cols].astype(F32)
        upd[:, cols] = (feats[h].astype(F32) + BRANCH * total).astype(BF16)
    blocks = dot(upd[...], weight_ref[...], 1, 0)
    width = blocks.shape[1]
    species = species_ref[...]
    lanes = jnp.zeros_like(species)
    for s in range(orbitals_ref.shape[0]):
        lanes = jnp.where(species == s, orbitals_ref[s], lanes)
    square = [lax.broadcasted_iota(jnp.int32, (atoms, atoms), d) for d in (0, 1)]
    norb = jnp.sum(jnp.where(square[0] == square[1], lanes, 0), axis=1, keepdims=True)
    cols = core * width + lax.broadcasted_iota(jnp.int32, (atoms, width), 1)
    valid = ((cols // (2 * ORB)) < norb) & (((cols // 2) % ORB) < norb)
    error = jnp.where(valid, blocks - target_ref[...], 0.0)
    divisor = norb.astype(F32)
    loss_ref[...] = jnp.sum(error * error, axis=1, keepdims=True) / divisor
    dblk = (2.0 * error / divisor).astype(BF16)
    parts = load_ref.shape[0]
    share = 2 * half // parts
    for g in range(parts):
        where = (g % 2) * (parts // 2) + g // 2
        load_ref[where, :, :width] = dblk
        load_ref[where, :, width : width + share] = upd[:, g * share : (g + 1) * share]
        load_ref[where, :, width + share :] = jnp.zeros((atoms, width - share), BF16)
    keep_ref[...] = dot(dblk, weight_ref[pl.ds(pl.multiple_of(core * half, 128), half), :], 1, 1)
    send_ref[...] = dot(dblk, weight_ref[pl.ds(pl.multiple_of((1 - core) * half, 128), half), :], 1, 1).astype(BF16)


def head(core, orbitals, species, f_own, f_oth, mine, recv, weight, target, parts):
    atoms, half = f_own.shape
    smem = pl.BlockSpec(memory_space=pltpu.SMEM)
    vmem = pl.BlockSpec(memory_space=pltpu.VMEM)
    return pl.pallas_call(
        head_kernel,
        out_shape=(
            jax.ShapeDtypeStruct((parts, atoms, 2 * target.shape[1]), BF16),
            jax.ShapeDtypeStruct((atoms, 1), F32),
            jax.ShapeDtypeStruct((atoms, half), F32),
            jax.ShapeDtypeStruct((atoms, half), BF16),
        ),
        in_specs=[smem, smem] + [vmem] * 7,
        out_specs=(vmem,) * 4,
        scratch_shapes=[
            pltpu.VMEM((2, atoms, half), BF16),
            pltpu.VMEM((atoms, 2 * half), BF16),
        ],
        compiler_params=pltpu.CompilerParams(vmem_limit_bytes=32 * 1024 * 1024),
        cost_estimate=pl.CostEstimate(flops=300_000_000, bytes_accessed=6_000_000, transcendentals=0),
        name="head",
    )(core, orbitals, species.reshape(1, -1), f_own, f_oth, mine, recv, weight, target)


def leaving_kernel(sends_ref, feats_ref, *outs):
    atoms = feats_ref.shape[0]
    places = lax.broadcasted_iota(jnp.int32, (atoms, atoms), 0)
    picks = jnp.concatenate(
        [(sends_ref[q : q + 1, :] == places).astype(F32) for q in range(len(outs))], axis=1
    ).astype(BF16)
    rows = dot(picks, feats_ref[...], 0, 0).astype(BF16)
    for q, out in enumerate(outs):
        out[...] = rows[q * atoms : (q + 1) * atoms, :]


def leaving_rows(send_rows, features):
    vmem = pl.BlockSpec(memory_space=pltpu.VMEM)
    return pl.pallas_call(
        leaving_kernel,
        out_shape=(jax.ShapeDtypeStruct(features.shape, BF16),) * len(OFFSETS),
        in_specs=[vmem, vmem],
        out_specs=(vmem,) * len(OFFSETS),
        compiler_params=pltpu.CompilerParams(vmem_limit_bytes=24 * 1024 * 1024),
        name="leaving",
    )(send_rows, features)


def partial_kernel(got_ref, out_ref):
    width = got_ref.shape[1] // 2
    full = dot(got_ref[:, width:], got_ref[:, :width], 0, 0)
    out_ref[...] = full[: out_ref.shape[0]].astype(BF16)


def partial_grad(got, share):
    vmem = pl.BlockSpec(memory_space=pltpu.VMEM)
    return pl.pallas_call(
        partial_kernel,
        out_shape=jax.ShapeDtypeStruct((share, got.shape[1] // 2), BF16),
        in_specs=[vmem],
        out_specs=vmem,
        compiler_params=pltpu.CompilerParams(vmem_limit_bytes=24 * 1024 * 1024),
        name="partial_grad",
    )(got)


def shift(x, axis, by):
    count = lax.axis_size(axis)
    return lax.ppermute(x, axis, [(i, (i + by) % count) for i in range(count)])


def plane_shift(x, early, by):
    pairs = []
    for y in range(4):
        for x_at in range(4):
            for c in range(2):
                along_x = (c == 0) == early
                to = (y, (x_at + by) % 4) if along_x else ((y + by) % 4, x_at)
                pairs.append(((y * 4 + x_at) * 2 + c, (to[0] * 4 + to[1]) * 2 + c))
    return lax.ppermute(x, ("y", "x", "chan"), pairs)


def assemble_kernel(lates, place_ref, *refs):
    halves, out_ref, sems = refs[: 2 * len(lates)], refs[-2], refs[-1]
    y, x, core = place_ref[0], place_ref[1], place_ref[2]
    rows = out_ref.shape[0] // 16
    copies = []
    for i, late in enumerate(lates):
        for early in range(4):
            dy = late + core * (early - late)
            dx = early + core * (late - early)
            spot = lax.rem(y + 4 - dy, 4) * 4 + lax.rem(x + 4 - dx, 4)
            copies.append(
                pltpu.make_async_copy(
                    halves[2 * i + early // 2].at[pl.ds(early % 2 * rows, rows), :],
                    out_ref.at[pl.ds(pl.multiple_of(spot * rows, 16), rows), :],
                    sems.at[len(copies)],
                )
            )
    for copy in copies:
        copy.start()
    for copy in copies:
        copy.wait()


def assemble(place, lates, halves, into=None):
    rows, width = halves[0].shape
    hbm = pl.BlockSpec(memory_space=pl.ANY)
    given = [] if into is None else [into]
    return pl.pallas_call(
        functools.partial(assemble_kernel, lates),
        out_shape=jax.ShapeDtypeStruct((8 * rows, width), BF16),
        in_specs=[pl.BlockSpec(memory_space=pltpu.SMEM)]
        + [pl.BlockSpec(memory_space=pltpu.VMEM)] * len(halves)
        + [hbm] * len(given),
        out_specs=hbm,
        input_output_aliases={1 + len(halves): 0} if given else {},
        scratch_shapes=[pltpu.SemaphoreType.DMA((4 * len(lates),))],
        compiler_params=pltpu.CompilerParams(vmem_limit_bytes=16 * 1024 * 1024),
        name="assemble",
    )(place, *halves, *given)


def body(
    features, send_rows, edge_source, edge_dest, edge_rot, edge_weight, rot_table,
    mix_zero, mix_one, mix_two, atom_species, species_orbitals, head_weight, target_blocks,
):
    core = lax.axis_index("chan").astype(jnp.int32).reshape(1)
    leaving = leaving_rows(send_rows, features)
    halo = [shift(leaving[OFFSETS.index(off)], ATOMS, off) for off in HALO_ORDER]
    prepared = prepare(
        edge_source, edge_dest, edge_rot, edge_weight, rot_table.T,
        (mix_zero, mix_one, mix_two), features.shape[0],
    )
    features, prepared = lax.optimization_barrier((features, prepared))
    f_oth = shift(features, "chan", 1)
    halo_oth = [shift(h, "chan", 1) for h in halo]
    mine = messages(core, prepared, [features] + halo, [f_oth] + halo_oth)
    recv = shift(mine, "chan", 1)
    parts = lax.axis_size(GROUP)
    load, loss, keep, send = head(
        core, species_orbitals, atom_species, features, f_oth, mine, recv, head_weight, target_blocks, parts
    )
    got = lax.all_to_all(load, GROUP, split_axis=0, concat_axis=0, tiled=True)
    share = 2 * features.shape[1] // parts
    part = partial_grad(got.reshape(-1, got.shape[2]), share)
    part, loss, send = lax.optimization_barrier((part, loss, send))
    sums = [shift(part, "zh", by) for by in (1, -1, 2)]
    loss_oth, feat_oth = shift(loss[:, 0], "chan", 1), shift(send, "chan", 1)
    sums, loss_oth, feat_oth = lax.optimization_barrier((sums, loss_oth, feat_oth))
    near = sums[0].astype(F32) + sums[1].astype(F32)
    total = (part.astype(F32) + sums[2].astype(F32) + near).astype(BF16)
    atom_loss = loss[:, 0] + loss_oth
    grad_features = keep + feat_oth.astype(F32)
    twin = shift(total, "zl", 1)
    first = lax.axis_index("zl") == 0
    pair = jnp.concatenate([jnp.where(first, total, twin), jnp.where(first, twin, total)], axis=0)

    early = {by: plane_shift(pair, True, by) for by in (1, -1, 2)}
    low = jnp.concatenate([pair, early[1]], axis=0)
    low_behind = plane_shift(low, False, 1)
    low_ahead = plane_shift(low, False, -1)
    high = jnp.concatenate([early[2], early[-1]], axis=0)
    high_ahead = plane_shift(high, False, -1)
    high_behind = plane_shift(high, False, 1)
    low_far = plane_shift(low_behind, False, 1)
    high_far = plane_shift(high_ahead, False, -1)
    place = jnp.stack([lax.axis_index(name) for name in ("y", "x", "chan")]).astype(jnp.int32)
    grad_head = assemble(
        place, (0, 1, 3), [low, high, low_behind, high_behind, low_ahead, high_ahead]
    )
    grad_head = assemble(place, (2,), [low_far, high_far], grad_head)
    return (atom_loss, grad_head, grad_features)


def solution(mesh):
    fine = Mesh(mesh.devices.reshape(4, 2, 4, 4, 2), ("zh", "zl", "y", "x", "chan"))
    both = ATOMS + ("chan",)
    return jax.shard_map(
        body,
        mesh=fine,
        in_specs=(
            P(ATOMS, "chan"), P(ATOMS, None), P(both), P(both), P(both), P(both),
            P(), P(), P(), P(), P(ATOMS), P(), P(None, "chan"), P(ATOMS, "chan"),
        ),
        out_specs=(P(ATOMS), P(None, "chan"), P(ATOMS, "chan")),
        check_vma=False,
    )
```

```python
import functools
import jax
import jax.numpy as jnp
import numpy as np
from jax import lax
from jax.experimental import pallas as pl
from jax.experimental.pallas import tpu as pltpu
from jax.sharding import Mesh, PartitionSpec as P

ORB = 16
LMAX = 4
MMAX = 2
OFFSETS = (1, -1, 2, -2)
HALO_ORDER = (1, 2, -1, -2)
BRANCH = 0.125
PREP_MB = 56
MSG_MB = 52
GROUP = ("zl", "y", "x")
ATOMS = ("zh", "zl", "y", "x")
F32 = jnp.float32
BF16 = jnp.bfloat16


def frame_entries():
    slots = {}
    start = 0
    for l in range(LMAX + 1):
        width = 2 * l + 1
        for m in range(-min(l, MMAX), min(l, MMAX) + 1):
            for n in range(width):
                slots[(l, m, n)] = (len(slots), start + (l + m) * width + n)
        start += width * width
    return slots


SLOTS = frame_entries()


def dot(a, b, ca, cb):
    return lax.dot_general(a, b, (((ca,), (cb,)), ((), ())), preferred_element_type=F32)


def prepare_kernel(
    esrc_hbm, edst_hbm, erot_hbm, ew_hbm, rot_hbm, mix0_hbm, mix1_hbm, mix2_hbm,
    frames, wframes, mix0_ref, mix1_ref, mix2_ref,
    packed, esrc_ref, edst_ref, erot_ref, ew_ref, rot_ref, mix0_in, mix1_in, mix2_in, sems,
):
    copies = [
        pltpu.make_async_copy(src, dst, sems.at[i])
        for i, (src, dst) in enumerate(
            (
                (erot_hbm, erot_ref), (ew_hbm, ew_ref), (rot_hbm, rot_ref), (esrc_hbm, esrc_ref),
                (edst_hbm, edst_ref), (mix0_hbm, mix0_in), (mix1_hbm, mix1_in), (mix2_hbm, mix2_in),
            )
        )
    ]
    for copy in copies:
        copy.start()
    for copy in copies[:5]:
        copy.wait()
    edges = esrc_ref.shape[1]

    depth, width = mix0_in.shape
    atoms = (mix0_ref.shape[0] - depth) // 6
    mix0_ref[depth:, edges:] = jnp.zeros((6 * atoms, width - edges), BF16)
    for ids, start, count in ((esrc_ref, depth, 5 * atoms), (edst_ref, depth + 5 * atoms, atoms)):
        places = lax.broadcasted_iota(jnp.int32, (count, edges), 0)
        mix0_ref[start : start + count, :edges] = (ids[...] == places).astype(BF16)

    rot_count = rot_ref.shape[1]
    picks = (erot_ref[...] == lax.broadcasted_iota(jnp.int32, (rot_count, edges), 0)).astype(BF16)
    rot = rot_ref[...]
    rot_hi = rot.astype(BF16)
    rot_lo = (rot - rot_hi.astype(F32)).astype(BF16)
    packed[...] = dot(rot_hi, picks, 1, 0) + dot(rot_lo, picks, 1, 0)
    for blk in range(edges // 128):
        lanes = slice(blk * 128, (blk + 1) * 128)
        weight = jnp.broadcast_to(ew_ref[:, lanes], (8, 128))
        for slot, entry in SLOTS.values():
            value = jnp.broadcast_to(packed[entry : entry + 1, lanes], (8, 128))
            frames[blk, slot] = value
            wframes[blk, slot] = value * weight

    for copy in copies[5:]:
        copy.wait()
    mix0_ref[:depth, :] = mix0_in[...].T
    for i in range(2):
        mix1_ref[i] = mix1_in[i].T
        mix2_ref[i] = mix2_in[i].T


def prepare(esrc, edst, erot, ew, rot_table, mixes, atoms):
    edges = esrc.shape[-1]
    row = lambda a: a.reshape(1, -1)
    vmem = pl.BlockSpec(memory_space=pltpu.VMEM)
    frames = jax.ShapeDtypeStruct((edges // 128, len(SLOTS), 8, 128), F32)
    return pl.pallas_call(
        prepare_kernel,
        out_shape=(frames, frames, jax.ShapeDtypeStruct((mixes[0].shape[0] + 6 * atoms, mixes[0].shape[1]), BF16))
        + tuple(jax.ShapeDtypeStruct(mix.shape, BF16) for mix in mixes[1:]),
        in_specs=[pl.BlockSpec(memory_space=pl.ANY)] * 8,
        out_specs=(vmem,) * 5,
        scratch_shapes=[pltpu.VMEM((rot_table.shape[0], edges), F32)]
        + [pltpu.VMEM((1, edges), jnp.int32)] * 3
        + [pltpu.VMEM((1, edges), F32), pltpu.VMEM(rot_table.shape, F32)]
        + [pltpu.VMEM(mix.shape, BF16) for mix in mixes]
        + [pltpu.SemaphoreType.DMA((8,))],
        compiler_params=pltpu.CompilerParams(vmem_limit_bytes=PREP_MB * 1024 * 1024),
        cost_estimate=pl.CostEstimate(flops=100_000_000, bytes_accessed=10_000_000, transcendentals=0),
        name="prepare",
    )(row(esrc), row(edst), row(erot), row(ew), rot_table, *mixes)


def message_kernel(
    core_ref, frames_hbm, wframes_hbm, mix0_hbm, mix1_hbm, mix2_hbm,
    fo_ref, ho0_ref, ho1_ref, ho2_ref, ho3_ref,
    fx_ref, hx0_ref, hx1_ref, hx2_ref, hx3_ref,
    out_ref,
    rows, nat, z0, z1, z2, xb0, xb1, xb2,
    frames, wframes, mix0_ref, mix1_ref, mix2_ref, onehot_ref, scatter_ref, sems,
):
    core = core_ref[0]
    other = 1 - core
    depth, edges = mix0_ref.shape[0], onehot_ref.shape[1]
    pick_rows, place_rows = onehot_ref.shape[0], scatter_ref.shape[0]
    pick, frame, wframe, place, *mixes = [
        pltpu.make_async_copy(src, dst, sems.at[10 + i])
        for i, (src, dst) in enumerate(
            (
                (mix0_hbm.at[pl.ds(depth, pick_rows), pl.ds(0, edges)], onehot_ref),
                (frames_hbm, frames), (wframes_hbm, wframes),
                (mix0_hbm.at[pl.ds(depth + pick_rows, place_rows), pl.ds(0, edges)], scatter_ref),
                (mix0_hbm.at[pl.ds(0, depth), :], mix0_ref), (mix1_hbm, mix1_ref), (mix2_hbm, mix2_ref),
            )
        )
    ]
    atoms, half = fo_ref.shape

    moves = []
    for q, (own, oth) in enumerate(
        zip((fo_ref, ho0_ref, ho1_ref, ho2_ref, ho3_ref), (fx_ref, hx0_ref, hx1_ref, hx2_ref, hx3_ref))
    ):
        at = pl.ds(0 if q == 0 else (1 + OFFSETS.index(HALO_ORDER[q - 1])) * atoms, atoms)
        moves.append(pltpu.make_async_copy(own, rows.at[core, at, :], sems.at[2 * q]))
        moves.append(pltpu.make_async_copy(oth, rows.at[other, at, :], sems.at[2 * q + 1]))
    for move in [pick] + moves + [frame] + mixes + [wframe, place]:
        move.start()
    pick.wait()
    onehot = onehot_ref[...]

    step = 640

    def gather(i, _):
        h = i // (half // step)
        n = i % (half // step)
        got = dot(rows[h, :, pl.ds(pl.multiple_of(n * step, 128), step)], onehot, 0, 0)
        at = pl.multiple_of(i * step, 8)
        for blk in range(edges // 128):
            nat[blk, pl.ds(at, step), :] = got[:, blk * 128 : (blk + 1) * 128]
        return 0

    for move in moves:
        move.wait()
    lax.fori_loop(0, 2 * half // step, gather, 0, unroll=10)

    groups = 2 * half // 400

    def rotate_in(i, _):
        blk = i // groups
        g = i % groups
        for p in range(2):
            nb = blk * 2 + p
            for l in range(LMAX + 1):
                xs = [nat[blk, pl.ds(g * 400 + p * 25 + l * l + n, 8, stride=50), :] for n in range(2 * l + 1)]
                for m in range(-min(l, MMAX), min(l, MMAX) + 1):
                    acc = frames[blk, SLOTS[(l, m, 0)][0]] * xs[0]
                    for n in range(1, 2 * l + 1):
                        acc = acc + frames[blk, SLOTS[(l, m, n)][0]] * xs[n]
                    if m == 0:
                        z0[nb, pl.ds(g * 40 + l, 8, stride=5), :] = acc
                    else:
                        side = nb if m > 0 else nb + 4
                        if abs(m) == 1:
                            z1[side, pl.ds(g * 32 + l - 1, 8, stride=4), :] = acc
                        else:
                            z2[side, pl.ds(g * 24 + l - 2, 8, stride=3), :] = acc
        return 0

    frame.wait()
    lax.fori_loop(0, groups * (edges // 128), rotate_in, 0, unroll=4)

    for nb in range(4):
        xb0[:, nb * 128 : (nb + 1) * 128] = z0[nb].astype(BF16)
    for nb in range(8):
        xb1[:, nb * 128 : (nb + 1) * 128] = z1[nb].astype(BF16)
        xb2[:, nb * 128 : (nb + 1) * 128] = z2[nb].astype(BF16)

    def mix_zero(n, _):
        y = dot(mix0_ref[...], xb0[:, pl.ds(pl.multiple_of(n * 256, 256), 256)], 1, 0)
        z0[2 * n] = y[:, :128]
        z0[2 * n + 1] = y[:, 128:]
        return 0

    for mix in mixes:
        mix.wait()
    lax.fori_loop(0, 2, mix_zero, 0, unroll=True)

    def mix_pair(mix_ref, xb, z):
        def part(n, _):
            plus = xb[:, pl.ds(pl.multiple_of(n * 256, 256), 256)]
            minus = xb[:, pl.ds(pl.multiple_of(n * 256 + 512, 256), 256)]
            y = dot(mix_ref[0], plus, 1, 0) - dot(mix_ref[1], minus, 1, 0)
            z[2 * n] = y[:, :128]
            z[2 * n + 1] = y[:, 128:]
            y = dot(mix_ref[0], minus, 1, 0) + dot(mix_ref[1], plus, 1, 0)
            z[2 * n + 4] = y[:, :128]
            z[2 * n + 5] = y[:, 128:]
            return 0

        lax.fori_loop(0, 2, part, 0, unroll=True)

    mix_pair(mix1_ref, xb1, z1)
    mix_pair(mix2_ref, xb2, z2)

    def rotate_out(i, _):
        blk = i // groups
        g = i % groups
        for p in range(2):
            nb = blk * 2 + p
            for l in range(LMAX + 1):
                ms = range(-min(l, MMAX), min(l, MMAX) + 1)
                ys = {}
                for m in ms:
                    side = nb if m >= 0 else nb + 4
                    if m == 0:
                        ys[m] = z0[nb, pl.ds(g * 40 + l, 8, stride=5), :]
                    elif abs(m) == 1:
                        ys[m] = z1[side, pl.ds(g * 32 + l - 1, 8, stride=4), :]
                    else:
                        ys[m] = z2[side, pl.ds(g * 24 + l - 2, 8, stride=3), :]
                for n in range(2 * l + 1):
                    acc = None
                    for m in ms:
                        term = wframes[blk, SLOTS[(l, m, n)][0]] * ys[m]
                        acc = term if acc is None else acc + term
                    nat[blk, pl.ds(g * 400 + p * 25 + l * l + n, 8, stride=50), :] = acc
        return 0

    wframe.wait()
    lax.fori_loop(0, groups * (edges // 128), rotate_out, 0)
    place.wait()

    scatter = scatter_ref[...]

    def aggregate(i, _):
        at = pl.multiple_of(i * step, 128)
        msgs = jnp.concatenate(
            [nat[blk, pl.ds(at, step), :].astype(BF16) for blk in range(edges // 128)], axis=1
        )
        out_ref[:, pl.ds(at, step)] = dot(scatter, msgs, 1, 1).astype(BF16)
        return 0

    lax.fori_loop(0, 2 * half // step, aggregate, 0, unroll=5)


def messages(core, prepared, own, oth):
    frames, wframes, mix0, mix1, mix2 = prepared
    atoms, half = own[0].shape
    edges = 128 * frames.shape[0]
    depth = mix0.shape[0] - 6 * atoms
    vmem = pl.BlockSpec(memory_space=pltpu.VMEM)
    return pl.pallas_call(
        message_kernel,
        out_shape=jax.ShapeDtypeStruct((atoms, 2 * half), BF16),
        in_specs=[pl.BlockSpec(memory_space=pltpu.SMEM)]
        + [pl.BlockSpec(memory_space=pl.ANY)] * (len(prepared) + 10),
        out_specs=vmem,
        scratch_shapes=[
            pltpu.VMEM((2, 5 * atoms, half), BF16),
            pltpu.VMEM((edges // 128, 2 * half, 128), F32),
            pltpu.VMEM((4, 640, 128), F32),
            pltpu.VMEM((8, 512, 128), F32),
            pltpu.VMEM((8, 384, 128), F32),
            pltpu.VMEM((640, 512), BF16),
            pltpu.VMEM((512, 1024), BF16),
            pltpu.VMEM((384, 1024), BF16),
        ]
        + [pltpu.VMEM(frames.shape, F32)] * 2
        + [pltpu.VMEM((depth, depth), BF16), pltpu.VMEM(mix1.shape, BF16), pltpu.VMEM(mix2.shape, BF16)]
        + [pltpu.VMEM((5 * atoms, edges), BF16), pltpu.VMEM((atoms, edges), BF16)]
        + [pltpu.SemaphoreType.DMA((17,))],
        compiler_params=pltpu.CompilerParams(vmem_limit_bytes=MSG_MB * 1024 * 1024),
        cost_estimate=pl.CostEstimate(flops=5_000_000_000, bytes_accessed=6_000_000, transcendentals=0),
        name="messages",
    )(core, *prepared, *own, *oth)


def head_kernel(
    core_ref, orbitals_ref, species_ref, fo_ref, fx_ref, mine_ref, recv_ref, weight_ref, target_ref,
    load_ref, loss_ref, keep_ref, send_ref,
    feats, upd,
):
    core = core_ref[0]
    atoms, half = fo_ref.shape
    feats[core] = fo_ref[...]
    feats[1 - core] = fx_ref[...]
    for h in range(2):
        cols = slice(h * half, (h + 1) * half)
        total = mine_ref[:, cols].astype(F32) + recv_ref[:, cols].astype(F32)
        upd[:, cols] = (feats[h].astype(F32) + BRANCH * total).astype(BF16)
    blocks = dot(upd[...], weight_ref[...], 1, 0)
    width = blocks.shape[1]
    species = species_ref[...]
    lanes = jnp.zeros_like(species)
    for s in range(orbitals_ref.shape[0]):
        lanes = jnp.where(species == s, orbitals_ref[s], lanes)
    square = [lax.broadcasted_iota(jnp.int32, (atoms, atoms), d) for d in (0, 1)]
    norb = jnp.sum(jnp.where(square[0] == square[1], lanes, 0), axis=1, keepdims=True)
    cols = core * width + lax.broadcasted_iota(jnp.int32, (atoms, width), 1)
    valid = ((cols // (2 * ORB)) < norb) & (((cols // 2) % ORB) < norb)
    error = jnp.where(valid, blocks - target_ref[...], 0.0)
    divisor = norb.astype(F32)
    loss_ref[...] = jnp.sum(error * error, axis=1, keepdims=True) / divisor
    dblk = (2.0 * error / divisor).astype(BF16)
    parts = load_ref.shape[0]
    share = 2 * half // parts
    for g in range(parts):
        where = (g % 2) * (parts // 2) + g // 2
        load_ref[where, :, :width] = dblk
        load_ref[where, :, width : width + share] = upd[:, g * share : (g + 1) * share]
        load_ref[where, :, width + share :] = jnp.zeros((atoms, width - share), BF16)
    keep_ref[...] = dot(dblk, weight_ref[pl.ds(pl.multiple_of(core * half, 128), half), :], 1, 1)
    send_ref[...] = dot(dblk, weight_ref[pl.ds(pl.multiple_of((1 - core) * half, 128), half), :], 1, 1).astype(BF16)


def head(core, orbitals, species, f_own, f_oth, mine, recv, weight, target, parts):
    atoms, half = f_own.shape
    smem = pl.BlockSpec(memory_space=pltpu.SMEM)
    vmem = pl.BlockSpec(memory_space=pltpu.VMEM)
    return pl.pallas_call(
        head_kernel,
        out_shape=(
            jax.ShapeDtypeStruct((parts, atoms, 2 * target.shape[1]), BF16),
            jax.ShapeDtypeStruct((atoms, 1), F32),
            jax.ShapeDtypeStruct((atoms, half), F32),
            jax.ShapeDtypeStruct((atoms, half), BF16),
        ),
        in_specs=[smem, smem] + [vmem] * 7,
        out_specs=(vmem,) * 4,
        scratch_shapes=[
            pltpu.VMEM((2, atoms, half), BF16),
            pltpu.VMEM((atoms, 2 * half), BF16),
        ],
        compiler_params=pltpu.CompilerParams(vmem_limit_bytes=32 * 1024 * 1024),
        cost_estimate=pl.CostEstimate(flops=300_000_000, bytes_accessed=6_000_000, transcendentals=0),
        name="head",
    )(core, orbitals, species.reshape(1, -1), f_own, f_oth, mine, recv, weight, target)


def leaving_kernel(sends_ref, feats_ref, *outs):
    atoms = feats_ref.shape[0]
    places = lax.broadcasted_iota(jnp.int32, (atoms, atoms), 0)
    picks = jnp.concatenate(
        [(sends_ref[q : q + 1, :] == places).astype(F32) for q in range(len(outs))], axis=1
    ).astype(BF16)
    rows = dot(picks, feats_ref[...], 0, 0).astype(BF16)
    for q, out in enumerate(outs):
        out[...] = rows[q * atoms : (q + 1) * atoms, :]


def leaving_rows(send_rows, features):
    vmem = pl.BlockSpec(memory_space=pltpu.VMEM)
    return pl.pallas_call(
        leaving_kernel,
        out_shape=(jax.ShapeDtypeStruct(features.shape, BF16),) * len(OFFSETS),
        in_specs=[vmem, vmem],
        out_specs=(vmem,) * len(OFFSETS),
        compiler_params=pltpu.CompilerParams(vmem_limit_bytes=24 * 1024 * 1024),
        name="leaving",
    )(send_rows, features)


def partial_kernel(got_ref, out_ref):
    width = got_ref.shape[1] // 2
    full = dot(got_ref[:, width:], got_ref[:, :width], 0, 0)
    out_ref[...] = full[: out_ref.shape[0]].astype(BF16)


def partial_grad(got, share):
    vmem = pl.BlockSpec(memory_space=pltpu.VMEM)
    return pl.pallas_call(
        partial_kernel,
        out_shape=jax.ShapeDtypeStruct((share, got.shape[1] // 2), BF16),
        in_specs=[vmem],
        out_specs=vmem,
        compiler_params=pltpu.CompilerParams(vmem_limit_bytes=24 * 1024 * 1024),
        name="partial_grad",
    )(got)


def shift(x, axis, by):
    count = lax.axis_size(axis)
    return lax.ppermute(x, axis, [(i, (i + by) % count) for i in range(count)])


def plane_shift(x, early, by):
    pairs = []
    for y in range(4):
        for x_at in range(4):
            for c in range(2):
                along_x = (c == 0) == early
                to = (y, (x_at + by) % 4) if along_x else ((y + by) % 4, x_at)
                pairs.append(((y * 4 + x_at) * 2 + c, (to[0] * 4 + to[1]) * 2 + c))
    return lax.ppermute(x, ("y", "x", "chan"), pairs)


def assemble_kernel(lates, place_ref, *refs):
    halves, out_ref, sems = refs[: 2 * len(lates)], refs[-2], refs[-1]
    y, x, core = place_ref[0], place_ref[1], place_ref[2]
    rows = out_ref.shape[0] // 16
    copies = []
    for i, late in enumerate(lates):
        for early in range(4):
            dy = late + core * (early - late)
            dx = early + core * (late - early)
            spot = lax.rem(y + 4 - dy, 4) * 4 + lax.rem(x + 4 - dx, 4)
            copies.append(
                pltpu.make_async_copy(
                    halves[2 * i + early // 2].at[pl.ds(early % 2 * rows, rows), :],
                    out_ref.at[pl.ds(pl.multiple_of(spot * rows, 16), rows), :],
                    sems.at[len(copies)],
                )
            )
    for copy in copies:
        copy.start()
    for copy in copies:
        copy.wait()


def assemble(place, lates, halves, into=None):
    rows, width = halves[0].shape
    hbm = pl.BlockSpec(memory_space=pl.ANY)
    given = [] if into is None else [into]
    return pl.pallas_call(
        functools.partial(assemble_kernel, lates),
        out_shape=jax.ShapeDtypeStruct((8 * rows, width), BF16),
        in_specs=[pl.BlockSpec(memory_space=pltpu.SMEM)]
        + [pl.BlockSpec(memory_space=pltpu.VMEM)] * len(halves)
        + [hbm] * len(given),
        out_specs=hbm,
        input_output_aliases={1 + len(halves): 0} if given else {},
        scratch_shapes=[pltpu.SemaphoreType.DMA((4 * len(lates),))],
        compiler_params=pltpu.CompilerParams(vmem_limit_bytes=16 * 1024 * 1024),
        name="assemble",
    )(place, *halves, *given)


def body(
    features, send_rows, edge_source, edge_dest, edge_rot, edge_weight, rot_table,
    mix_zero, mix_one, mix_two, atom_species, species_orbitals, head_weight, target_blocks,
):
    core = lax.axis_index("chan").astype(jnp.int32).reshape(1)
    leaving = leaving_rows(send_rows, features)
    halo = [shift(leaving[OFFSETS.index(off)], ATOMS, off) for off in HALO_ORDER]
    prepared = prepare(
        edge_source, edge_dest, edge_rot, edge_weight, rot_table.T,
        (mix_zero, mix_one, mix_two), features.shape[0],
    )
    features, prepared = lax.optimization_barrier((features, prepared))
    f_oth = shift(features, "chan", 1)
    halo_oth = [shift(h, "chan", 1) for h in halo]
    mine = messages(core, prepared, [features] + halo, [f_oth] + halo_oth)
    recv = shift(mine, "chan", 1)
    parts = lax.axis_size(GROUP)
    load, loss, keep, send = head(
        core, species_orbitals, atom_species, features, f_oth, mine, recv, head_weight, target_blocks, parts
    )
    got = lax.all_to_all(load, GROUP, split_axis=0, concat_axis=0, tiled=True)
    share = 2 * features.shape[1] // parts
    part = partial_grad(got.reshape(-1, got.shape[2]), share)
    part, loss, send = lax.optimization_barrier((part, loss, send))
    sums = [shift(part, "zh", by) for by in (1, -1, 2)]
    loss_oth, feat_oth = shift(loss[:, 0], "chan", 1), shift(send, "chan", 1)
    sums, loss_oth, feat_oth = lax.optimization_barrier((sums, loss_oth, feat_oth))
    near = sums[0].astype(F32) + sums[1].astype(F32)
    total = (part.astype(F32) + sums[2].astype(F32) + near).astype(BF16)
    atom_loss = loss[:, 0] + loss_oth
    grad_features = keep + feat_oth.astype(F32)
    twin = shift(total, "zl", 1)
    first = lax.axis_index("zl") == 0
    pair = jnp.concatenate([jnp.where(first, total, twin), jnp.where(first, twin, total)], axis=0)

    early = {by: plane_shift(pair, True, by) for by in (1, -1, 2)}
    low = jnp.concatenate([pair, early[1]], axis=0)
    low_behind = plane_shift(low, False, 1)
    low_ahead = plane_shift(low, False, -1)
    high = jnp.concatenate([early[2], early[-1]], axis=0)
    high_ahead = plane_shift(high, False, -1)
    high_behind = plane_shift(high, False, 1)
    low_far = plane_shift(low_behind, False, 1)
    high_far = plane_shift(high_ahead, False, -1)
    place = jnp.stack([lax.axis_index(name) for name in ("y", "x", "chan")]).astype(jnp.int32)
    grad_head = assemble(
        place, (0, 1, 3), [low, high, low_behind, high_behind, low_ahead, high_ahead]
    )
    grad_head = assemble(place, (2,), [low_far, high_far], grad_head)
    return (atom_loss, grad_head, grad_features)


def solution(mesh):
    fine = Mesh(mesh.devices.reshape(4, 2, 4, 4, 2), ("zh", "zl", "y", "x", "chan"))
    both = ATOMS + ("chan",)
    return jax.shard_map(
        body,
        mesh=fine,
        in_specs=(
            P(ATOMS, "chan"), P(ATOMS, None), P(both), P(both), P(both), P(both),
            P(), P(), P(), P(), P(ATOMS), P(), P(None, "chan"), P(ATOMS, "chan"),
        ),
        out_specs=(P(ATOMS), P(None, "chan"), P(ATOMS, "chan")),
        check_vma=False,
    )
```

```python
import functools
import jax
import jax.numpy as jnp
import numpy as np
from jax import lax
from jax.experimental import pallas as pl
from jax.experimental.pallas import tpu as pltpu
from jax.sharding import Mesh, PartitionSpec as P

ORB = 16
LMAX = 4
MMAX = 2
OFFSETS = (1, -1, 2, -2)
BRANCH = 0.125
PREP_MB = 56
MSG_MB = 54
GROUP = ("zl", "y", "x")
ATOMS = ("zh", "zl", "y", "x")
F32 = jnp.float32
BF16 = jnp.bfloat16


def frame_entries():
    slots = {}
    start = 0
    for l in range(LMAX + 1):
        width = 2 * l + 1
        for m in range(-min(l, MMAX), min(l, MMAX) + 1):
            for n in range(width):
                slots[(l, m, n)] = (len(slots), start + (l + m) * width + n)
        start += width * width
    return slots


SLOTS = frame_entries()


def dot(a, b, ca, cb):
    return lax.dot_general(a, b, (((ca,), (cb,)), ((), ())), preferred_element_type=F32)


def prepare_kernel(
    esrc_hbm, edst_hbm, erot_hbm, ew_hbm, rot_hbm, mix0_hbm, mix1_hbm, mix2_hbm,
    frames, wframes, onehot_ref, scatter_ref, mix0_ref, mix1_ref, mix2_ref,
    packed, esrc_ref, edst_ref, erot_ref, ew_ref, rot_ref, mix0_in, mix1_in, mix2_in, sems,
):
    copies = [
        pltpu.make_async_copy(src, dst, sems.at[i])
        for i, (src, dst) in enumerate(
            (
                (erot_hbm, erot_ref), (ew_hbm, ew_ref), (rot_hbm, rot_ref), (esrc_hbm, esrc_ref),
                (edst_hbm, edst_ref), (mix0_hbm, mix0_in), (mix1_hbm, mix1_in), (mix2_hbm, mix2_in),
            )
        )
    ]
    for copy in copies:
        copy.start()
    for copy in copies[:5]:
        copy.wait()
    edges = esrc_ref.shape[1]

    onehot_ref[...] = (esrc_ref[...] == lax.broadcasted_iota(jnp.int32, onehot_ref.shape, 0)).astype(BF16)
    scatter_ref[...] = (edst_ref[...] == lax.broadcasted_iota(jnp.int32, scatter_ref.shape, 0)).astype(BF16)

    rot_count = rot_ref.shape[1]
    picks = (erot_ref[...] == lax.broadcasted_iota(jnp.int32, (rot_count, edges), 0)).astype(BF16)
    rot = rot_ref[...]
    rot_hi = rot.astype(BF16)
    rot_lo = (rot - rot_hi.astype(F32)).astype(BF16)
    packed[...] = dot(rot_hi, picks, 1, 0) + dot(rot_lo, picks, 1, 0)
    for blk in range(edges // 128):
        lanes = slice(blk * 128, (blk + 1) * 128)
        weight = jnp.broadcast_to(ew_ref[:, lanes], (8, 128))
        for slot, entry in SLOTS.values():
            value = jnp.broadcast_to(packed[entry : entry + 1, lanes], (8, 128))
            frames[blk, slot] = value
            wframes[blk, slot] = value * weight

    for copy in copies[5:]:
        copy.wait()
    mix0_ref[...] = mix0_in[...].T
    for i in range(2):
        mix1_ref[i] = mix1_in[i].T
        mix2_ref[i] = mix2_in[i].T


def prepare(esrc, edst, erot, ew, rot_table, mixes, atoms):
    edges = esrc.shape[-1]
    row = lambda a: a.reshape(1, -1)
    vmem = pl.BlockSpec(memory_space=pltpu.VMEM)
    frames = jax.ShapeDtypeStruct((edges // 128, len(SLOTS), 8, 128), F32)
    return pl.pallas_call(
        prepare_kernel,
        out_shape=(
            frames, frames,
            jax.ShapeDtypeStruct((5 * atoms, edges), BF16),
            jax.ShapeDtypeStruct((atoms, edges), BF16),
        )
        + tuple(jax.ShapeDtypeStruct(mix.shape, BF16) for mix in mixes),
        in_specs=[pl.BlockSpec(memory_space=pl.ANY)] * 8,
        out_specs=(vmem,) * 7,
        scratch_shapes=[pltpu.VMEM((rot_table.shape[0], edges), F32)]
        + [pltpu.VMEM((1, edges), jnp.int32)] * 3
        + [pltpu.VMEM((1, edges), F32), pltpu.VMEM(rot_table.shape, F32)]
        + [pltpu.VMEM(mix.shape, BF16) for mix in mixes]
        + [pltpu.SemaphoreType.DMA((8,))],
        compiler_params=pltpu.CompilerParams(vmem_limit_bytes=PREP_MB * 1024 * 1024),
        cost_estimate=pl.CostEstimate(flops=100_000_000, bytes_accessed=10_000_000, transcendentals=0),
        name="prepare",
    )(row(esrc), row(edst), row(erot), row(ew), rot_table, *mixes)


def message_kernel(
    core_ref, frames_hbm, wframes_hbm, onehot_hbm, scatter_hbm, mix0_hbm, mix1_hbm, mix2_hbm,
    fo_ref, ho0_ref, ho1_ref, ho2_ref, ho3_ref,
    fx_ref, hx0_ref, hx1_ref, hx2_ref, hx3_ref,
    out_ref,
    rows, nat, z0, z1, z2, xb0, xb1, xb2,
    frames, wframes, onehot_ref, scatter_ref, mix0_ref, mix1_ref, mix2_ref, sems,
):
    core = core_ref[0]
    other = 1 - core
    pick, frame, wframe, place, *mixes = [
        pltpu.make_async_copy(src, dst, sems.at[10 + i])
        for i, (src, dst) in enumerate(
            (
                (onehot_hbm, onehot_ref), (frames_hbm, frames), (wframes_hbm, wframes),
                (scatter_hbm, scatter_ref), (mix0_hbm, mix0_ref), (mix1_hbm, mix1_ref), (mix2_hbm, mix2_ref),
            )
        )
    ]
    edges = onehot_ref.shape[1]
    atoms, half = fo_ref.shape

    moves = []
    for q, (own, oth) in enumerate(
        zip((fo_ref, ho0_ref, ho1_ref, ho2_ref, ho3_ref), (fx_ref, hx0_ref, hx1_ref, hx2_ref, hx3_ref))
    ):
        slot = 0 if q == 0 else 1 + core_ref[q]
        at = pl.ds(pl.multiple_of(slot * atoms, 32), atoms)
        moves.append(pltpu.make_async_copy(own, rows.at[core, at, :], sems.at[2 * q]))
        moves.append(pltpu.make_async_copy(oth, rows.at[other, at, :], sems.at[2 * q + 1]))
    for move in [pick] + moves + [frame] + mixes + [wframe, place]:
        move.start()
    pick.wait()
    onehot = onehot_ref[...]

    step = 640

    def gather(i, _):
        h = i // (half // step)
        n = i % (half // step)
        got = dot(rows[h, :, pl.ds(pl.multiple_of(n * step, 128), step)], onehot, 0, 0)
        at = pl.multiple_of(i * step, 8)
        for blk in range(edges // 128):
            nat[blk, pl.ds(at, step), :] = got[:, blk * 128 : (blk + 1) * 128]
        return 0

    for move in moves:
        move.wait()
    lax.fori_loop(0, 2 * half // step, gather, 0, unroll=10)

    groups = 2 * half // 400

    def rotate_in(i, _):
        blk = i // groups
        g = i % groups
        for p in range(2):
            nb = blk * 2 + p
            for l in range(LMAX + 1):
                xs = [nat[blk, pl.ds(g * 400 + p * 25 + l * l + n, 8, stride=50), :] for n in range(2 * l + 1)]
                for m in range(-min(l, MMAX), min(l, MMAX) + 1):
                    acc = frames[blk, SLOTS[(l, m, 0)][0]] * xs[0]
                    for n in range(1, 2 * l + 1):
                        acc = acc + frames[blk, SLOTS[(l, m, n)][0]] * xs[n]
                    if m == 0:
                        z0[nb, pl.ds(g * 40 + l, 8, stride=5), :] = acc
                    else:
                        side = nb if m > 0 else nb + 4
                        if abs(m) == 1:
                            z1[side, pl.ds(g * 32 + l - 1, 8, stride=4), :] = acc
                        else:
                            z2[side, pl.ds(g * 24 + l - 2, 8, stride=3), :] = acc
        return 0

    frame.wait()
    lax.fori_loop(0, groups * (edges // 128), rotate_in, 0, unroll=4)

    for nb in range(4):
        xb0[:, nb * 128 : (nb + 1) * 128] = z0[nb].astype(BF16)
    for nb in range(8):
        xb1[:, nb * 128 : (nb + 1) * 128] = z1[nb].astype(BF16)
        xb2[:, nb * 128 : (nb + 1) * 128] = z2[nb].astype(BF16)

    def mix_zero(n, _):
        y = dot(mix0_ref[...], xb0[:, pl.ds(pl.multiple_of(n * 256, 256), 256)], 1, 0)
        z0[2 * n] = y[:, :128]
        z0[2 * n + 1] = y[:, 128:]
        return 0

    for mix in mixes:
        mix.wait()
    lax.fori_loop(0, 2, mix_zero, 0, unroll=True)

    def mix_pair(mix_ref, xb, z):
        def part(n, _):
            plus = xb[:, pl.ds(pl.multiple_of(n * 256, 256), 256)]
            minus = xb[:, pl.ds(pl.multiple_of(n * 256 + 512, 256), 256)]
            y = dot(mix_ref[0], plus, 1, 0) - dot(mix_ref[1], minus, 1, 0)
            z[2 * n] = y[:, :128]
            z[2 * n + 1] = y[:, 128:]
            y = dot(mix_ref[0], minus, 1, 0) + dot(mix_ref[1], plus, 1, 0)
            z[2 * n + 4] = y[:, :128]
            z[2 * n + 5] = y[:, 128:]
            return 0

        lax.fori_loop(0, 2, part, 0, unroll=True)

    mix_pair(mix1_ref, xb1, z1)
    mix_pair(mix2_ref, xb2, z2)

    def rotate_out(i, _):
        blk = i // groups
        g = i % groups
        for p in range(2):
            nb = blk * 2 + p
            for l in range(LMAX + 1):
                ms = range(-min(l, MMAX), min(l, MMAX) + 1)
                ys = {}
                for m in ms:
                    side = nb if m >= 0 else nb + 4
                    if m == 0:
                        ys[m] = z0[nb, pl.ds(g * 40 + l, 8, stride=5), :]
                    elif abs(m) == 1:
                        ys[m] = z1[side, pl.ds(g * 32 + l - 1, 8, stride=4), :]
                    else:
                        ys[m] = z2[side, pl.ds(g * 24 + l - 2, 8, stride=3), :]
                for n in range(2 * l + 1):
                    acc = None
                    for m in ms:
                        term = wframes[blk, SLOTS[(l, m, n)][0]] * ys[m]
                        acc = term if acc is None else acc + term
                    nat[blk, pl.ds(g * 400 + p * 25 + l * l + n, 8, stride=50), :] = acc
        return 0

    wframe.wait()
    lax.fori_loop(0, groups * (edges // 128), rotate_out, 0)
    place.wait()

    scatter = scatter_ref[...]

    def aggregate(i, _):
        at = pl.multiple_of(i * step, 128)
        msgs = jnp.concatenate(
            [nat[blk, pl.ds(at, step), :].astype(BF16) for blk in range(edges // 128)], axis=1
        )
        out_ref[:, pl.ds(at, step)] = dot(scatter, msgs, 1, 1).astype(BF16)
        return 0

    lax.fori_loop(0, 2 * half // step, aggregate, 0, unroll=5)


def messages(core, prepared, own, oth):
    edges = prepared[2].shape[1]
    atoms, half = own[0].shape
    vmem = pl.BlockSpec(memory_space=pltpu.VMEM)
    return pl.pallas_call(
        message_kernel,
        out_shape=jax.ShapeDtypeStruct((atoms, 2 * half), BF16),
        in_specs=[pl.BlockSpec(memory_space=pltpu.SMEM)]
        + [pl.BlockSpec(memory_space=pl.ANY)] * (len(prepared) + 10),
        out_specs=vmem,
        scratch_shapes=[
            pltpu.VMEM((2, 5 * atoms, half), BF16),
            pltpu.VMEM((edges // 128, 2 * half, 128), F32),
            pltpu.VMEM((4, 640, 128), F32),
            pltpu.VMEM((8, 512, 128), F32),
            pltpu.VMEM((8, 384, 128), F32),
            pltpu.VMEM((640, 512), BF16),
            pltpu.VMEM((512, 1024), BF16),
            pltpu.VMEM((384, 1024), BF16),
        ]
        + [pltpu.VMEM(table.shape, table.dtype) for table in prepared]
        + [pltpu.SemaphoreType.DMA((17,))],
        compiler_params=pltpu.CompilerParams(vmem_limit_bytes=MSG_MB * 1024 * 1024),
        cost_estimate=pl.CostEstimate(flops=5_000_000_000, bytes_accessed=6_000_000, transcendentals=0),
        name="messages",
    )(core, *prepared, *own, *oth)


def head_kernel(
    core_ref, orbitals_ref, species_ref, fo_ref, fx_ref, mine_ref, recv_ref, weight_ref, target_ref,
    load_ref, loss_ref, keep_ref, send_ref,
    feats, upd,
):
    core = core_ref[0]
    atoms, half = fo_ref.shape
    feats[core] = fo_ref[...]
    feats[1 - core] = fx_ref[...]
    for h in range(2):
        cols = slice(h * half, (h + 1) * half)
        total = mine_ref[:, cols].astype(F32) + recv_ref[:, cols].astype(F32)
        upd[:, cols] = (feats[h].astype(F32) + BRANCH * total).astype(BF16)
    blocks = dot(upd[...], weight_ref[...], 1, 0)
    width = blocks.shape[1]
    species = species_ref[...]
    lanes = jnp.zeros_like(species)
    for s in range(orbitals_ref.shape[0]):
        lanes = jnp.where(species == s, orbitals_ref[s], lanes)
    square = [lax.broadcasted_iota(jnp.int32, (atoms, atoms), d) for d in (0, 1)]
    norb = jnp.sum(jnp.where(square[0] == square[1], lanes, 0), axis=1, keepdims=True)
    cols = core * width + lax.broadcasted_iota(jnp.int32, (atoms, width), 1)
    valid = ((cols // (2 * ORB)) < norb) & (((cols // 2) % ORB) < norb)
    error = jnp.where(valid, blocks - target_ref[...], 0.0)
    divisor = norb.astype(F32)
    loss_ref[...] = jnp.sum(error * error, axis=1, keepdims=True) / divisor
    dblk = (2.0 * error / divisor).astype(BF16)
    parts = load_ref.shape[0]
    share = 2 * half // parts
    for g in range(parts):
        where = (g % 2) * (parts // 2) + g // 2
        load_ref[where, :, :width] = dblk
        load_ref[where, :, width : width + share] = upd[:, g * share : (g + 1) * share]
        load_ref[where, :, width + share :] = jnp.zeros((atoms, width - share), BF16)
    keep_ref[...] = dot(dblk, weight_ref[pl.ds(pl.multiple_of(core * half, 128), half), :], 1, 1)
    send_ref[...] = dot(dblk, weight_ref[pl.ds(pl.multiple_of((1 - core) * half, 128), half), :], 1, 1).astype(BF16)


def head(core, orbitals, species, f_own, f_oth, mine, recv, weight, target, parts):
    atoms, half = f_own.shape
    smem = pl.BlockSpec(memory_space=pltpu.SMEM)
    vmem = pl.BlockSpec(memory_space=pltpu.VMEM)
    return pl.pallas_call(
        head_kernel,
        out_shape=(
            jax.ShapeDtypeStruct((parts, atoms, 2 * target.shape[1]), BF16),
            jax.ShapeDtypeStruct((atoms, 1), F32),
            jax.ShapeDtypeStruct((atoms, half), F32),
            jax.ShapeDtypeStruct((atoms, half), BF16),
        ),
        in_specs=[smem, smem] + [vmem] * 7,
        out_specs=(vmem,) * 4,
        scratch_shapes=[
            pltpu.VMEM((2, atoms, half), BF16),
            pltpu.VMEM((atoms, 2 * half), BF16),
        ],
        compiler_params=pltpu.CompilerParams(vmem_limit_bytes=32 * 1024 * 1024),
        cost_estimate=pl.CostEstimate(flops=300_000_000, bytes_accessed=6_000_000, transcendentals=0),
        name="head",
    )(core, orbitals, species.reshape(1, -1), f_own, f_oth, mine, recv, weight, target)


def leaving_kernel(order_ref, sends_ref, feats_ref, *outs):
    atoms = feats_ref.shape[0]
    places = lax.broadcasted_iota(jnp.int32, (atoms, atoms), 0)
    picks = jnp.concatenate(
        [(sends_ref[pl.ds(order_ref[q], 1), :] == places).astype(F32) for q in range(len(outs))], axis=1
    ).astype(BF16)
    rows = dot(picks, feats_ref[...], 0, 0).astype(BF16)
    for q, out in enumerate(outs):
        out[...] = rows[q * atoms : (q + 1) * atoms, :]


def leaving_rows(order, send_rows, features):
    vmem = pl.BlockSpec(memory_space=pltpu.VMEM)
    return pl.pallas_call(
        leaving_kernel,
        out_shape=(jax.ShapeDtypeStruct(features.shape, BF16),) * len(OFFSETS),
        in_specs=[pl.BlockSpec(memory_space=pltpu.SMEM), vmem, vmem],
        out_specs=(vmem,) * len(OFFSETS),
        compiler_params=pltpu.CompilerParams(vmem_limit_bytes=24 * 1024 * 1024),
        name="leaving",
    )(order, send_rows, features)


def partial_kernel(got_ref, out_ref):
    width = got_ref.shape[1] // 2
    full = dot(got_ref[:, width:], got_ref[:, :width], 0, 0)
    out_ref[...] = full[: out_ref.shape[0]].astype(BF16)


def partial_grad(got, share):
    vmem = pl.BlockSpec(memory_space=pltpu.VMEM)
    return pl.pallas_call(
        partial_kernel,
        out_shape=jax.ShapeDtypeStruct((share, got.shape[1] // 2), BF16),
        in_specs=[vmem],
        out_specs=vmem,
        compiler_params=pltpu.CompilerParams(vmem_limit_bytes=24 * 1024 * 1024),
        name="partial_grad",
    )(got)


def shift(x, axis, by):
    count = lax.axis_size(axis)
    return lax.ppermute(x, axis, [(i, (i + by) % count) for i in range(count)])


def plane_shift(x, early, by):
    pairs = []
    for y in range(4):
        for x_at in range(4):
            for c in range(2):
                along_x = (c == 0) == early
                to = (y, (x_at + by) % 4) if along_x else ((y + by) % 4, x_at)
                pairs.append(((y * 4 + x_at) * 2 + c, (to[0] * 4 + to[1]) * 2 + c))
    return lax.ppermute(x, ("y", "x", "chan"), pairs)


def assemble_kernel(lates, place_ref, *refs):
    halves, out_ref, sems = refs[: 2 * len(lates)], refs[-2], refs[-1]
    y, x, core = place_ref[0], place_ref[1], place_ref[2]
    rows = out_ref.shape[0] // 16
    copies = []
    for i, late in enumerate(lates):
        for early in range(4):
            dy = late + core * (early - late)
            dx = early + core * (late - early)
            spot = lax.rem(y + 4 - dy, 4) * 4 + lax.rem(x + 4 - dx, 4)
            copies.append(
                pltpu.make_async_copy(
                    halves[2 * i + early // 2].at[pl.ds(early % 2 * rows, rows), :],
                    out_ref.at[pl.ds(pl.multiple_of(spot * rows, 16), rows), :],
                    sems.at[len(copies)],
                )
            )
    for copy in copies:
        copy.start()
    for copy in copies:
        copy.wait()


def assemble(place, lates, halves, into=None):
    rows, width = halves[0].shape
    hbm = pl.BlockSpec(memory_space=pl.ANY)
    given = [] if into is None else [into]
    return pl.pallas_call(
        functools.partial(assemble_kernel, lates),
        out_shape=jax.ShapeDtypeStruct((8 * rows, width), BF16),
        in_specs=[pl.BlockSpec(memory_space=pltpu.SMEM)]
        + [pl.BlockSpec(memory_space=pltpu.VMEM)] * len(halves)
        + [hbm] * len(given),
        out_specs=hbm,
        input_output_aliases={1 + len(halves): 0} if given else {},
        scratch_shapes=[pltpu.SemaphoreType.DMA((4 * len(lates),))],
        compiler_params=pltpu.CompilerParams(vmem_limit_bytes=16 * 1024 * 1024),
        name="assemble",
    )(place, *halves, *given)


def body(
    features, send_rows, edge_source, edge_dest, edge_rot, edge_weight, rot_table,
    mix_zero, mix_one, mix_two, atom_species, species_orbitals, head_weight, target_blocks,
):
    core = lax.axis_index("chan").astype(jnp.int32).reshape(1)
    count = lax.axis_size(ATOMS)
    me = lax.axis_index(ATOMS)
    swaps = []
    for later in (False, True):
        for step in (1, 2):
            to = [i + step if (i // step % 2 == 0) != later else i - step for i in range(count)]
            forward = (me // step % 2 == 0) != later
            ahead, back = OFFSETS.index(step), OFFSETS.index(-step)
            swaps.append(([(i, t % count) for i, t in enumerate(to)], jnp.where(forward, ahead, back), ahead + back))
    sent = jnp.stack([q for _, q, _ in swaps]).astype(jnp.int32)
    got_from = jnp.stack([both - q for _, q, both in swaps]).astype(jnp.int32)
    leaving = leaving_rows(sent, send_rows, features)
    halo = [lax.ppermute(rows, ATOMS, pairs) for rows, (pairs, _, _) in zip(leaving, swaps)]
    prepared = prepare(
        edge_source, edge_dest, edge_rot, edge_weight, rot_table.T,
        (mix_zero, mix_one, mix_two), features.shape[0],
    )
    features, prepared = lax.optimization_barrier((features, prepared))
    f_oth = shift(features, "chan", 1)
    halo_oth = [shift(h, "chan", 1) for h in halo]
    mine = messages(jnp.concatenate([core, got_from]), prepared, [features] + halo, [f_oth] + halo_oth)
    recv = shift(mine, "chan", 1)
    parts = lax.axis_size(GROUP)
    load, loss, keep, send = head(
        core, species_orbitals, atom_species, features, f_oth, mine, recv, head_weight, target_blocks, parts
    )
    got = lax.all_to_all(load, GROUP, split_axis=0, concat_axis=0, tiled=True)
    share = 2 * features.shape[1] // parts
    part = partial_grad(got.reshape(-1, got.shape[2]), share)
    part, loss, send = lax.optimization_barrier((part, loss, send))
    sums = [shift(part, "zh", by) for by in (1, -1, 2)]
    loss_oth, feat_oth = shift(loss[:, 0], "chan", 1), shift(send, "chan", 1)
    sums, loss_oth, feat_oth = lax.optimization_barrier((sums, loss_oth, feat_oth))
    near = sums[0].astype(F32) + sums[1].astype(F32)
    total = (part.astype(F32) + sums[2].astype(F32) + near).astype(BF16)
    atom_loss = loss[:, 0] + loss_oth
    grad_features = keep + feat_oth.astype(F32)
    twin = shift(total, "zl", 1)
    first = lax.axis_index("zl") == 0
    pair = jnp.concatenate([jnp.where(first, total, twin), jnp.where(first, twin, total)], axis=0)

    early = {by: plane_shift(pair, True, by) for by in (1, -1, 2)}
    low = jnp.concatenate([pair, early[1]], axis=0)
    low_behind = plane_shift(low, False, 1)
    low_ahead = plane_shift(low, False, -1)
    high = jnp.concatenate([early[2], early[-1]], axis=0)
    high_ahead = plane_shift(high, False, -1)
    high_behind = plane_shift(high, False, 1)
    low_far = plane_shift(low_behind, False, 1)
    high_far = plane_shift(high_ahead, False, -1)
    place = jnp.stack([lax.axis_index(name) for name in ("y", "x", "chan")]).astype(jnp.int32)
    grad_head = assemble(
        place, (0, 1, 3), [low, high, low_behind, high_behind, low_ahead, high_ahead]
    )
    grad_head = assemble(place, (2,), [low_far, high_far], grad_head)
    return (atom_loss, grad_head, grad_features)


def solution(mesh):
    fine = Mesh(mesh.devices.reshape(4, 2, 4, 4, 2), ("zh", "zl", "y", "x", "chan"))
    both = ATOMS + ("chan",)
    return jax.shard_map(
        body,
        mesh=fine,
        in_specs=(
            P(ATOMS, "chan"), P(ATOMS, None), P(both), P(both), P(both), P(both),
            P(), P(), P(), P(), P(ATOMS), P(), P(None, "chan"), P(ATOMS, "chan"),
        ),
        out_specs=(P(ATOMS), P(None, "chan"), P(ATOMS, "chan")),
        check_vma=False,
    )
```

```python
import functools
import jax
import jax.numpy as jnp
import numpy as np
from jax import lax
from jax.experimental import pallas as pl
from jax.experimental.pallas import tpu as pltpu
from jax.sharding import Mesh, PartitionSpec as P

ORB = 16
LMAX = 4
MMAX = 2
OFFSETS = (1, -1, 2, -2)
HALO_ORDER = (1, 2, -1, -2)
BRANCH = 0.125
PREP_MB = 56
MSG_MB = 54
GROUP = ("zl", "y", "x")
ATOMS = ("zh", "zl", "y", "x")
F32 = jnp.float32
BF16 = jnp.bfloat16


def frame_entries():
    slots = {}
    start = 0
    for l in range(LMAX + 1):
        width = 2 * l + 1
        for m in range(-min(l, MMAX), min(l, MMAX) + 1):
            for n in range(width):
                slots[(l, m, n)] = (len(slots), start + (l + m) * width + n)
        start += width * width
    return slots


SLOTS = frame_entries()


def dot(a, b, ca, cb):
    return lax.dot_general(a, b, (((ca,), (cb,)), ((), ())), preferred_element_type=F32)


def prepare_kernel(
    esrc_hbm, edst_hbm, erot_hbm, ew_hbm, rot_hbm, mix0_hbm, mix1_hbm, mix2_hbm,
    frames, wframes, onehot_ref, scatter_ref, mix0_ref, mix1_ref, mix2_ref,
    packed, esrc_ref, edst_ref, erot_ref, ew_ref, rot_ref, mix0_in, mix1_in, mix2_in, sems,
):
    copies = [
        pltpu.make_async_copy(src, dst, sems.at[i])
        for i, (src, dst) in enumerate(
            (
                (erot_hbm, erot_ref), (ew_hbm, ew_ref), (rot_hbm, rot_ref), (esrc_hbm, esrc_ref),
                (edst_hbm, edst_ref), (mix0_hbm, mix0_in), (mix1_hbm, mix1_in), (mix2_hbm, mix2_in),
            )
        )
    ]
    for copy in copies:
        copy.start()
    for copy in copies[:5]:
        copy.wait()
    edges = esrc_ref.shape[1]

    onehot_ref[...] = (esrc_ref[...] == lax.broadcasted_iota(jnp.int32, onehot_ref.shape, 0)).astype(BF16)
    scatter_ref[...] = (edst_ref[...] == lax.broadcasted_iota(jnp.int32, scatter_ref.shape, 0)).astype(BF16)

    rot_count = rot_ref.shape[1]
    picks = (erot_ref[...] == lax.broadcasted_iota(jnp.int32, (rot_count, edges), 0)).astype(BF16)
    rot = rot_ref[...]
    rot_hi = rot.astype(BF16)
    rot_lo = (rot - rot_hi.astype(F32)).astype(BF16)
    packed[...] = dot(rot_hi, picks, 1, 0) + dot(rot_lo, picks, 1, 0)
    for blk in range(edges // 128):
        lanes = slice(blk * 128, (blk + 1) * 128)
        weight = jnp.broadcast_to(ew_ref[:, lanes], (8, 128))
        for slot, entry in SLOTS.values():
            value = jnp.broadcast_to(packed[entry : entry + 1, lanes], (8, 128))
            frames[blk, slot] = value
            wframes[blk, slot] = value * weight

    for copy in copies[5:]:
        copy.wait()
    mix0_ref[...] = mix0_in[...].T
    for i in range(2):
        mix1_ref[i] = mix1_in[i].T
        mix2_ref[i] = mix2_in[i].T


def prepare(esrc, edst, erot, ew, rot_table, mixes, atoms):
    edges = esrc.shape[-1]
    row = lambda a: a.reshape(1, -1)
    vmem = pl.BlockSpec(memory_space=pltpu.VMEM)
    frames = jax.ShapeDtypeStruct((edges // 128, len(SLOTS), 8, 128), F32)
    return pl.pallas_call(
        prepare_kernel,
        out_shape=(
            frames, frames,
            jax.ShapeDtypeStruct((5 * atoms, edges), BF16),
            jax.ShapeDtypeStruct((atoms, edges), BF16),
        )
        + tuple(jax.ShapeDtypeStruct(mix.shape, BF16) for mix in mixes),
        in_specs=[pl.BlockSpec(memory_space=pl.ANY)] * 8,
        out_specs=(vmem,) * 7,
        scratch_shapes=[pltpu.VMEM((rot_table.shape[0], edges), F32)]
        + [pltpu.VMEM((1, edges), jnp.int32)] * 3
        + [pltpu.VMEM((1, edges), F32), pltpu.VMEM(rot_table.shape, F32)]
        + [pltpu.VMEM(mix.shape, BF16) for mix in mixes]
        + [pltpu.SemaphoreType.DMA((8,))],
        compiler_params=pltpu.CompilerParams(vmem_limit_bytes=PREP_MB * 1024 * 1024),
        cost_estimate=pl.CostEstimate(flops=100_000_000, bytes_accessed=10_000_000, transcendentals=0),
        name="prepare",
    )(row(esrc), row(edst), row(erot), row(ew), rot_table, *mixes)


def message_kernel(
    core_ref, frames_hbm, wframes_hbm, onehot_hbm, scatter_hbm, mix0_hbm, mix1_hbm, mix2_hbm,
    fo_ref, ho0_ref, ho1_ref, ho2_ref, ho3_ref,
    fx_ref, hx0_ref, hx1_ref, hx2_ref, hx3_ref,
    out_ref,
    rows, nat, z0, z1, z2, xb0, xb1, xb2,
    frames, wframes, onehot_ref, scatter_ref, mix0_ref, mix1_ref, mix2_ref, sems,
):
    core = core_ref[0]
    other = 1 - core
    pick, frame, wframe, place, *mixes = [
        pltpu.make_async_copy(src, dst, sems.at[10 + i])
        for i, (src, dst) in enumerate(
            (
                (onehot_hbm, onehot_ref), (frames_hbm, frames), (wframes_hbm, wframes),
                (scatter_hbm, scatter_ref), (mix0_hbm, mix0_ref), (mix1_hbm, mix1_ref), (mix2_hbm, mix2_ref),
            )
        )
    ]
    edges = onehot_ref.shape[1]
    atoms, half = fo_ref.shape

    moves = []
    for q, (own, oth) in enumerate(
        zip((fo_ref, ho0_ref, ho1_ref, ho2_ref, ho3_ref), (fx_ref, hx0_ref, hx1_ref, hx2_ref, hx3_ref))
    ):
        at = pl.ds(0 if q == 0 else (1 + OFFSETS.index(HALO_ORDER[q - 1])) * atoms, atoms)
        moves.append(pltpu.make_async_copy(own, rows.at[core, at, :], sems.at[2 * q]))
        moves.append(pltpu.make_async_copy(oth, rows.at[other, at, :], sems.at[2 * q + 1]))
    for move in [pick] + moves + [frame] + mixes + [wframe, place]:
        move.start()
    pick.wait()
    onehot = onehot_ref[...]

    step = 640

    def gather(i, _):
        h = i // (half // step)
        n = i % (half // step)
        got = dot(rows[h, :, pl.ds(pl.multiple_of(n * step, 128), step)], onehot, 0, 0)
        at = pl.multiple_of(i * step, 8)
        for blk in range(edges // 128):
            nat[blk, pl.ds(at, step), :] = got[:, blk * 128 : (blk + 1) * 128]
        return 0

    for move in moves:
        move.wait()
    lax.fori_loop(0, 2 * half // step, gather, 0, unroll=10)

    groups = 2 * half // 400

    def rotate_in(i, _):
        blk = i // groups
        g = i % groups
        for p in range(2):
            nb = blk * 2 + p
            for l in range(LMAX + 1):
                xs = [nat[blk, pl.ds(g * 400 + p * 25 + l * l + n, 8, stride=50), :] for n in range(2 * l + 1)]
                for m in range(-min(l, MMAX), min(l, MMAX) + 1):
                    acc = frames[blk, SLOTS[(l, m, 0)][0]] * xs[0]
                    for n in range(1, 2 * l + 1):
                        acc = acc + frames[blk, SLOTS[(l, m, n)][0]] * xs[n]
                    if m == 0:
                        z0[nb, pl.ds(g * 40 + l, 8, stride=5), :] = acc
                    else:
                        side = nb if m > 0 else nb + 4
                        if abs(m) == 1:
                            z1[side, pl.ds(g * 32 + l - 1, 8, stride=4), :] = acc
                        else:
                            z2[side, pl.ds(g * 24 + l - 2, 8, stride=3), :] = acc
        return 0

    frame.wait()
    lax.fori_loop(0, groups * (edges // 128), rotate_in, 0, unroll=4)

    for nb in range(4):
        xb0[:, nb * 128 : (nb + 1) * 128] = z0[nb].astype(BF16)
    for nb in range(8):
        xb1[:, nb * 128 : (nb + 1) * 128] = z1[nb].astype(BF16)
        xb2[:, nb * 128 : (nb + 1) * 128] = z2[nb].astype(BF16)

    def mix_zero(n, _):
        y = dot(mix0_ref[...], xb0[:, pl.ds(pl.multiple_of(n * 256, 256), 256)], 1, 0)
        z0[2 * n] = y[:, :128]
        z0[2 * n + 1] = y[:, 128:]
        return 0

    for mix in mixes:
        mix.wait()
    lax.fori_loop(0, 2, mix_zero, 0, unroll=True)

    def mix_pair(mix_ref, xb, z):
        def part(n, _):
            plus = xb[:, pl.ds(pl.multiple_of(n * 256, 256), 256)]
            minus = xb[:, pl.ds(pl.multiple_of(n * 256 + 512, 256), 256)]
            y = dot(mix_ref[0], plus, 1, 0) - dot(mix_ref[1], minus, 1, 0)
            z[2 * n] = y[:, :128]
            z[2 * n + 1] = y[:, 128:]
            y = dot(mix_ref[0], minus, 1, 0) + dot(mix_ref[1], plus, 1, 0)
            z[2 * n + 4] = y[:, :128]
            z[2 * n + 5] = y[:, 128:]
            return 0

        lax.fori_loop(0, 2, part, 0, unroll=True)

    mix_pair(mix1_ref, xb1, z1)
    mix_pair(mix2_ref, xb2, z2)

    def rotate_out(i, _):
        blk = i // groups
        g = i % groups
        for p in range(2):
            nb = blk * 2 + p
            for l in range(LMAX + 1):
                ms = range(-min(l, MMAX), min(l, MMAX) + 1)
                ys = {}
                for m in ms:
                    side = nb if m >= 0 else nb + 4
                    if m == 0:
                        ys[m] = z0[nb, pl.ds(g * 40 + l, 8, stride=5), :]
                    elif abs(m) == 1:
                        ys[m] = z1[side, pl.ds(g * 32 + l - 1, 8, stride=4), :]
                    else:
                        ys[m] = z2[side, pl.ds(g * 24 + l - 2, 8, stride=3), :]
                for n in range(2 * l + 1):
                    acc = None
                    for m in ms:
                        term = wframes[blk, SLOTS[(l, m, n)][0]] * ys[m]
                        acc = term if acc is None else acc + term
                    nat[blk, pl.ds(g * 400 + p * 25 + l * l + n, 8, stride=50), :] = acc
        return 0

    wframe.wait()
    lax.fori_loop(0, groups * (edges // 128), rotate_out, 0)
    place.wait()

    scatter = scatter_ref[...]

    def aggregate(i, _):
        at = pl.multiple_of(i * step, 128)
        msgs = jnp.concatenate(
            [nat[blk, pl.ds(at, step), :].astype(BF16) for blk in range(edges // 128)], axis=1
        )
        out_ref[:, pl.ds(at, step)] = dot(scatter, msgs, 1, 1).astype(BF16)
        return 0

    lax.fori_loop(0, 2 * half // step, aggregate, 0, unroll=5)


def messages(core, prepared, own, oth):
    edges = prepared[2].shape[1]
    atoms, half = own[0].shape
    vmem = pl.BlockSpec(memory_space=pltpu.VMEM)
    return pl.pallas_call(
        message_kernel,
        out_shape=jax.ShapeDtypeStruct((atoms, 2 * half), BF16),
        in_specs=[pl.BlockSpec(memory_space=pltpu.SMEM)]
        + [pl.BlockSpec(memory_space=pl.ANY)] * (len(prepared) + 10),
        out_specs=vmem,
        scratch_shapes=[
            pltpu.VMEM((2, 5 * atoms, half), BF16),
            pltpu.VMEM((edges // 128, 2 * half, 128), F32),
            pltpu.VMEM((4, 640, 128), F32),
            pltpu.VMEM((8, 512, 128), F32),
            pltpu.VMEM((8, 384, 128), F32),
            pltpu.VMEM((640, 512), BF16),
            pltpu.VMEM((512, 1024), BF16),
            pltpu.VMEM((384, 1024), BF16),
        ]
        + [pltpu.VMEM(table.shape, table.dtype) for table in prepared]
        + [pltpu.SemaphoreType.DMA((17,))],
        compiler_params=pltpu.CompilerParams(vmem_limit_bytes=MSG_MB * 1024 * 1024),
        cost_estimate=pl.CostEstimate(flops=5_000_000_000, bytes_accessed=6_000_000, transcendentals=0),
        name="messages",
    )(core, *prepared, *own, *oth)


def head_kernel(
    core_ref, orbitals_ref, species_ref, fo_ref, fx_ref, mine_ref, recv_ref, weight_ref, target_ref,
    load_ref, loss_ref, keep_ref, send_ref,
    feats, upd,
):
    core = core_ref[0]
    atoms, half = fo_ref.shape
    feats[core] = fo_ref[...]
    feats[1 - core] = fx_ref[...]
    for h in range(2):
        cols = slice(h * half, (h + 1) * half)
        total = mine_ref[:, cols].astype(F32) + recv_ref[:, cols].astype(F32)
        upd[:, cols] = (feats[h].astype(F32) + BRANCH * total).astype(BF16)
    blocks = dot(upd[...], weight_ref[...], 1, 0)
    width = blocks.shape[1]
    species = species_ref[...]
    lanes = jnp.zeros_like(species)
    for s in range(orbitals_ref.shape[0]):
        lanes = jnp.where(species == s, orbitals_ref[s], lanes)
    square = [lax.broadcasted_iota(jnp.int32, (atoms, atoms), d) for d in (0, 1)]
    norb = jnp.sum(jnp.where(square[0] == square[1], lanes, 0), axis=1, keepdims=True)
    cols = core * width + lax.broadcasted_iota(jnp.int32, (atoms, width), 1)
    valid = ((cols // (2 * ORB)) < norb) & (((cols // 2) % ORB) < norb)
    error = jnp.where(valid, blocks - target_ref[...], 0.0)
    divisor = norb.astype(F32)
    loss_ref[...] = jnp.sum(error * error, axis=1, keepdims=True) / divisor
    dblk = (2.0 * error / divisor).astype(BF16)
    parts = load_ref.shape[0]
    share = 2 * half // parts
    for g in range(parts):
        where = (g % 2) * (parts // 2) + g // 2
        load_ref[where, :, :width] = dblk
        load_ref[where, :, width : width + share] = upd[:, g * share : (g + 1) * share]
        load_ref[where, :, width + share :] = jnp.zeros((atoms, width - share), BF16)
    keep_ref[...] = dot(dblk, weight_ref[pl.ds(pl.multiple_of(core * half, 128), half), :], 1, 1)
    send_ref[...] = dot(dblk, weight_ref[pl.ds(pl.multiple_of((1 - core) * half, 128), half), :], 1, 1).astype(BF16)


def head(core, orbitals, species, f_own, f_oth, mine, recv, weight, target, parts):
    atoms, half = f_own.shape
    smem = pl.BlockSpec(memory_space=pltpu.SMEM)
    vmem = pl.BlockSpec(memory_space=pltpu.VMEM)
    return pl.pallas_call(
        head_kernel,
        out_shape=(
            jax.ShapeDtypeStruct((parts, atoms, 2 * target.shape[1]), BF16),
            jax.ShapeDtypeStruct((atoms, 1), F32),
            jax.ShapeDtypeStruct((atoms, half), F32),
            jax.ShapeDtypeStruct((atoms, half), BF16),
        ),
        in_specs=[smem, smem] + [vmem] * 7,
        out_specs=(vmem,) * 4,
        scratch_shapes=[
            pltpu.VMEM((2, atoms, half), BF16),
            pltpu.VMEM((atoms, 2 * half), BF16),
        ],
        compiler_params=pltpu.CompilerParams(vmem_limit_bytes=32 * 1024 * 1024),
        cost_estimate=pl.CostEstimate(flops=300_000_000, bytes_accessed=6_000_000, transcendentals=0),
        name="head",
    )(core, orbitals, species.reshape(1, -1), f_own, f_oth, mine, recv, weight, target)


def leaving_kernel(sends_ref, feats_ref, *outs):
    atoms = feats_ref.shape[0]
    places = lax.broadcasted_iota(jnp.int32, (atoms, atoms), 0)
    picks = jnp.concatenate(
        [(sends_ref[q : q + 1, :] == places).astype(F32) for q in range(len(outs))], axis=1
    ).astype(BF16)
    rows = dot(picks, feats_ref[...], 0, 0).astype(BF16)
    for q, out in enumerate(outs):
        out[...] = rows[q * atoms : (q + 1) * atoms, :]


def leaving_rows(send_rows, features):
    vmem = pl.BlockSpec(memory_space=pltpu.VMEM)
    return pl.pallas_call(
        leaving_kernel,
        out_shape=(jax.ShapeDtypeStruct(features.shape, BF16),) * len(OFFSETS),
        in_specs=[vmem, vmem],
        out_specs=(vmem,) * len(OFFSETS),
        compiler_params=pltpu.CompilerParams(vmem_limit_bytes=24 * 1024 * 1024),
        name="leaving",
    )(send_rows, features)


def partial_kernel(got_ref, out_ref):
    width = got_ref.shape[1] // 2
    full = dot(got_ref[:, width:], got_ref[:, :width], 0, 0)
    out_ref[...] = full[: out_ref.shape[0]].astype(BF16)


def partial_grad(got, share):
    vmem = pl.BlockSpec(memory_space=pltpu.VMEM)
    return pl.pallas_call(
        partial_kernel,
        out_shape=jax.ShapeDtypeStruct((share, got.shape[1] // 2), BF16),
        in_specs=[vmem],
        out_specs=vmem,
        compiler_params=pltpu.CompilerParams(vmem_limit_bytes=24 * 1024 * 1024),
        name="partial_grad",
    )(got)


def shift(x, axis, by):
    count = lax.axis_size(axis)
    return lax.ppermute(x, axis, [(i, (i + by) % count) for i in range(count)])


def plane_shift(x, early, by):
    pairs = []
    for y in range(4):
        for x_at in range(4):
            for c in range(2):
                along_x = (c == 0) == early
                to = (y, (x_at + by) % 4) if along_x else ((y + by) % 4, x_at)
                pairs.append(((y * 4 + x_at) * 2 + c, (to[0] * 4 + to[1]) * 2 + c))
    return lax.ppermute(x, ("y", "x", "chan"), pairs)


def assemble_kernel(lates, place_ref, *refs):
    halves, out_ref, sems = refs[: 2 * len(lates)], refs[-2], refs[-1]
    y, x, core = place_ref[0], place_ref[1], place_ref[2]
    rows = out_ref.shape[0] // 16
    copies = []
    for i, late in enumerate(lates):
        for early in range(4):
            dy = late + core * (early - late)
            dx = early + core * (late - early)
            spot = lax.rem(y + 4 - dy, 4) * 4 + lax.rem(x + 4 - dx, 4)
            copies.append(
                pltpu.make_async_copy(
                    halves[2 * i + early // 2].at[pl.ds(early % 2 * rows, rows), :],
                    out_ref.at[pl.ds(pl.multiple_of(spot * rows, 16), rows), :],
                    sems.at[len(copies)],
                )
            )
    for copy in copies:
        copy.start()
    for copy in copies:
        copy.wait()


def assemble(place, lates, halves, into=None):
    rows, width = halves[0].shape
    hbm = pl.BlockSpec(memory_space=pl.ANY)
    given = [] if into is None else [into]
    return pl.pallas_call(
        functools.partial(assemble_kernel, lates),
        out_shape=jax.ShapeDtypeStruct((8 * rows, width), BF16),
        in_specs=[pl.BlockSpec(memory_space=pltpu.SMEM)]
        + [pl.BlockSpec(memory_space=pltpu.VMEM)] * len(halves)
        + [hbm] * len(given),
        out_specs=hbm,
        input_output_aliases={1 + len(halves): 0} if given else {},
        scratch_shapes=[pltpu.SemaphoreType.DMA((4 * len(lates),))],
        compiler_params=pltpu.CompilerParams(vmem_limit_bytes=16 * 1024 * 1024),
        name="assemble",
    )(place, *halves, *given)


def body(
    features, send_rows, edge_source, edge_dest, edge_rot, edge_weight, rot_table,
    mix_zero, mix_one, mix_two, atom_species, species_orbitals, head_weight, target_blocks,
):
    core = lax.axis_index("chan").astype(jnp.int32).reshape(1)
    leaving = leaving_rows(send_rows, features)
    halo = [shift(leaving[OFFSETS.index(off)], ATOMS, off) for off in HALO_ORDER]
    prepared = prepare(
        edge_source, edge_dest, edge_rot, edge_weight, rot_table.T,
        (mix_zero, mix_one, mix_two), features.shape[0],
    )
    features, prepared = lax.optimization_barrier((features, prepared))
    f_oth = shift(features, "chan", 1)
    halo_oth = [shift(h, "chan", 1) for h in halo]
    mine = messages(core, prepared, [features] + halo, [f_oth] + halo_oth)
    recv = shift(mine, "chan", 1)
    parts = lax.axis_size(GROUP)
    load, loss, keep, send = head(
        core, species_orbitals, atom_species, features, f_oth, mine, recv, head_weight, target_blocks, parts
    )
    got = lax.all_to_all(load, GROUP, split_axis=0, concat_axis=0, tiled=True)
    share = 2 * features.shape[1] // parts
    part = partial_grad(got.reshape(-1, got.shape[2]), share)
    part, loss, send = lax.optimization_barrier((part, loss, send))
    sums = [shift(part, "zh", by) for by in (2, 1, -1)]
    loss_oth, feat_oth = shift(loss[:, 0], "chan", 1), shift(send, "chan", 1)
    sums, loss_oth, feat_oth = lax.optimization_barrier((sums, loss_oth, feat_oth))
    near = sums[1].astype(F32) + sums[2].astype(F32)
    total = (part.astype(F32) + sums[0].astype(F32) + near).astype(BF16)
    atom_loss = loss[:, 0] + loss_oth
    grad_features = keep + feat_oth.astype(F32)
    twin = shift(total, "zl", 1)
    first = lax.axis_index("zl") == 0
    pair = jnp.concatenate([jnp.where(first, total, twin), jnp.where(first, twin, total)], axis=0)

    early = {by: plane_shift(pair, True, by) for by in (1, -1, 2)}
    low = jnp.concatenate([pair, early[1]], axis=0)
    low_behind = plane_shift(low, False, 1)
    low_ahead = plane_shift(low, False, -1)
    high = jnp.concatenate([early[2], early[-1]], axis=0)
    high_ahead = plane_shift(high, False, -1)
    high_behind = plane_shift(high, False, 1)
    low_far = plane_shift(low_behind, False, 1)
    high_far = plane_shift(high_ahead, False, -1)
    place = jnp.stack([lax.axis_index(name) for name in ("y", "x", "chan")]).astype(jnp.int32)
    grad_head = assemble(
        place, (0, 1, 3), [low, high, low_behind, high_behind, low_ahead, high_ahead]
    )
    grad_head = assemble(place, (2,), [low_far, high_far], grad_head)
    return (atom_loss, grad_head, grad_features)


def solution(mesh):
    fine = Mesh(mesh.devices.reshape(4, 2, 4, 4, 2), ("zh", "zl", "y", "x", "chan"))
    both = ATOMS + ("chan",)
    return jax.shard_map(
        body,
        mesh=fine,
        in_specs=(
            P(ATOMS, "chan"), P(ATOMS, None), P(both), P(both), P(both), P(both),
            P(), P(), P(), P(), P(ATOMS), P(), P(None, "chan"), P(ATOMS, "chan"),
        ),
        out_specs=(P(ATOMS), P(None, "chan"), P(ATOMS, "chan")),
        check_vma=False,
    )
```
